128 devices in a mesh: dp: 16 (over z, x), expert: 8 (over y, core).
Axes of the slice: x: 4, y: 4, z: 4, core: 2. Of those that a mesh axis runs over, the one named last changes fastest.
Arguments:
- local_grads: bfloat16 [16, 8, 4, 1048576], P('dp', 'expert')
- master_weights: float32 [8, 4, 1048576], P('expert', None, 'dp'), may hold values from -6 to 6
- first_moment: float32 [8, 4, 1048576], P('expert', None, 'dp')
- second_moment: float32 [8, 4, 1048576], P('expert', None, 'dp')
Outputs:
- new_params: bfloat16 [8, 4, 1048576], P('expert')
- new_master: float32 [8, 4, 1048576], P('expert', None, 'dp')
- new_first: float32 [8, 4, 1048576], P('expert', None, 'dp')
- new_second: float32 [8, 4, 1048576], P('expert', None, 'dp')
The draws below stay inside these ranges and needn't reach their ends.
All inputs are finite; a program needn't handle non-finite values.
Results may differ from the reference program's by a relative error of at most 0.0013.
Values may be sent and summed in bfloat16 or wider, within the bound.
No kernel may reach another device: no remote copies, remote signals or barrier semaphores. Data moves between devices by JAX's collectives and lax.ppermute only.
A program may use at most 128 MiB of HBM per device.

```python
import jax
import jax.numpy as jnp
from jax import lax

LAYERS = 4
SHARD = 65536
EXPERTS = 8
FLAT = 1048576
N_DP = 16


def unit_scale():
    return (EXPERTS * LAYERS * FLAT) ** (-0.5)


def profile_gains(key, block_top, jitter):
    replicas = FLAT // SHARD
    block_count = replicas * 4
    expert_rise = 1.0 + 2.0 * jnp.arange(EXPERTS, dtype=jnp.float32) / max(EXPERTS - 1, 1)
    expert_jitter = jnp.exp(jax.random.uniform(jax.random.fold_in(key, 11), (EXPERTS,), jnp.float32, -jitter, jitter))
    block_rise = 1.0 + block_top * jnp.arange(block_count, dtype=jnp.float32) / max(block_count - 1, 1)
    block_jitter = jnp.exp(jax.random.uniform(jax.random.fold_in(key, 12), (EXPERTS, LAYERS, block_count), jnp.float32, -jitter, jitter))
    blocks = (expert_rise * expert_jitter).reshape(EXPERTS, 1, 1) * block_rise.reshape(1, 1, block_count) * block_jitter
    return jnp.repeat(blocks, SHARD // 4, axis=2)


def draw_local_grads(key, part):
    replicas = FLAT // SHARD
    shape = (replicas, EXPERTS, LAYERS, FLAT)
    rough = jax.random.uniform(jax.random.fold_in(key, 7), (EXPERTS, LAYERS, FLAT), jnp.float32, 0.5, 1.5)
    gains = profile_gains(key, 2.0, 0.7)
    common = jax.random.normal(jax.random.fold_in(key, 3), (EXPERTS, LAYERS, FLAT), jnp.float32)
    single = jax.random.normal(jax.random.fold_in(key, 4), shape, jnp.float32)
    spread = 60.0
    centered = single - jnp.mean(single, axis=0, keepdims=True)
    values = (common[None] + spread * centered) * (gains * rough * unit_scale())[None]
    return values.astype(jnp.bfloat16)


def draw_first_moment(key, part):
    shape = (EXPERTS, LAYERS, FLAT)
    values = 0.3 * jax.random.normal(key, shape, jnp.float32)
    return values * unit_scale()


def draw_second_moment(key, part):
    shape = (EXPERTS, LAYERS, FLAT)
    low = 0.1
    logs = jax.random.uniform(key, shape, jnp.float32, jnp.log(low), 0.0)
    return jnp.exp(logs) * unit_scale() ** 2


def levels(own_key, extent, split, low, high):
    factor_of, own = 1.0, jax.random.fold_in(own_key, 6)
    for axis_at, shards_of in split:
        steps = jnp.exp(jax.random.uniform(jax.random.fold_in(own, axis_at), (shards_of,), jnp.float32, low / len(split), high / len(split)))
        factor_of = factor_of * jnp.repeat(steps, extent[axis_at] // shards_of).reshape([-1 if axis == axis_at else 1 for axis in range(len(extent))])
    return factor_of


def gaussian(own_key, shape, scale, bound, pieces=(), kind=jnp.bfloat16):
    gain = levels(own_key, shape, pieces, -0.22, 0.18) if pieces else 1.0
    result = jax.random.normal(own_key, shape, jnp.float32) * scale * gain
    return jnp.minimum(jnp.maximum(result, -bound), bound).astype(kind)


def setup_inputs(seed: int = 0) -> dict:
    key_of = jax.random.split(jax.random.key(seed), 5)
    local_grads = draw_local_grads(jax.random.fold_in(key_of[4], 71), 0)
    master_weights = gaussian(key_of[1], (EXPERTS, LAYERS, FLAT), 1.0, 6.0, ((0, 8), (2, 16)), jnp.float32)
    first_moment = draw_first_moment(jax.random.fold_in(key_of[4], 71), 0)
    second_moment = draw_second_moment(jax.random.fold_in(key_of[4], 71), 0)
    return dict(local_grads=local_grads, master_weights=master_weights, first_moment=first_moment, second_moment=second_moment)


beta_first = 0.9
beta_second = 0.95
correct_first = 1.0 - 0.9 ** 10
correct_second = 1.0 - 0.95 ** 10
learn_rate = 0.05
decay_rate = 0.1
clip_limit = 1.0
tiny_eps = 1e-08
norm_eps = 1e-06

def adam_update(gradient, master, first, second, clip_factor):
    scaled = clip_factor * gradient
    new_first = beta_first * first + (1.0 - beta_first) * scaled
    new_second = beta_second * second + (1.0 - beta_second) * scaled * scaled
    direction = new_first / correct_first / (jnp.sqrt(new_second / correct_second) + tiny_eps)
    new_master = master - learn_rate * (decay_rate * master + direction)
    return (new_master, new_first, new_second)

def reference(local_grads, master_weights, first_moment, second_moment):
    mean_grad = lax.optimization_barrier(jnp.sum(local_grads.astype(jnp.float32), axis=0)) / N_DP
    grad_norm = jnp.sqrt(jnp.sum(mean_grad * mean_grad))
    clip_factor = jnp.minimum(1.0, clip_limit / (grad_norm + norm_eps))
    new_master, new_first, new_second = adam_update(mean_grad, master_weights, first_moment, second_moment, clip_factor)
    return (new_master.astype(jnp.bfloat16), new_master, new_first, new_second)
```

```python
import functools

import jax
import jax.numpy as jnp
from jax import lax
from jax.experimental import pallas as pl
from jax.experimental.pallas import tpu as pltpu
from jax.sharding import Mesh
from jax.sharding import PartitionSpec as P

Z, X, Y, CORE = "z", "x", "y", "core"
beta_first = 0.9
beta_second = 0.95
correct_first = 1.0 - 0.9**10
correct_second = 1.0 - 0.95**10
learn_rate = 0.05
decay_rate = 0.1
clip_limit = 1.0
tiny_eps = 1e-08
norm_eps = 1e-06

LANES = 128
BLOCK = 256
VMEM_LIMIT = 12 * 2**20
f32, bf16 = jnp.float32, jnp.bfloat16


def shift(value, axis, by):
    size = lax.axis_size(axis)
    return lax.ppermute(value, axis, [(i, (i + by) % size) for i in range(size)])


def cost(flops, moved):
    return pl.CostEstimate(flops=flops, bytes_accessed=moved, transcendentals=0)


def first_sum_kernel(where, own, one, two, three, *outs):
    mine = where[1]
    for ahead, out in enumerate(outs):
        at = lax.rem(mine + ahead, 4)
        total = own[at].astype(f32)
        for part in (one, two, three):
            total += part[at].astype(f32)
        out[...] = total


def first_sum(pieces, arrived, where, along_z):
    half = arrived[0].shape[1]
    steps = half // BLOCK
    if along_z:
        own = pl.BlockSpec((None, 4, BLOCK, LANES), lambda i, w: (w[0], 0, i, 0))
    else:
        own = pl.BlockSpec((4, None, BLOCK, LANES), lambda i, w: (0, w[0], steps + i, 0))
    part = pl.BlockSpec((4, BLOCK, LANES), lambda i, w: (0, i, 0))
    out = pl.BlockSpec((BLOCK, LANES), lambda i, w: (i, 0))
    return pl.pallas_call(
        first_sum_kernel,
        grid_spec=pltpu.PrefetchScalarGridSpec(
            num_scalar_prefetch=1, grid=(steps,), in_specs=[own, part, part, part], out_specs=[out] * 4
        ),
        out_shape=[jax.ShapeDtypeStruct((half, LANES), f32)] * 4,
        compiler_params=pltpu.CompilerParams(vmem_limit_bytes=VMEM_LIMIT),
        cost_estimate=cost(16 * half * LANES, 4 * 4 * half * LANES * 3),
    )(where, pieces, *arrived)


def last_sum_kernel(*refs):
    parts_a, parts_b, (mean_a, mean_b, squares) = refs[:4], refs[4:8], refs[8:]

    @pl.when(pl.program_id(0) == 0)
    def _():
        squares[...] = jnp.zeros_like(squares)

    for parts, mean in ((parts_a, mean_a), (parts_b, mean_b)):
        total = (parts[0][...] + parts[1][...] + parts[2][...] + parts[3][...]) * (1.0 / 16.0)
        mean[...] = total
        squares[...] += jnp.sum((total * total).reshape(BLOCK // 8, 8, LANES), axis=0)


def last_sum(parts_a, parts_b):
    half = parts_a[0].shape[0]
    block = pl.BlockSpec((BLOCK, LANES), lambda i: (i, 0))
    return pl.pallas_call(
        last_sum_kernel,
        grid=(half // BLOCK,),
        in_specs=[block] * 8,
        out_specs=[block, block, pl.BlockSpec((8, LANES), lambda i: (0, 0))],
        out_shape=[jax.ShapeDtypeStruct((half, LANES), f32)] * 2 + [jax.ShapeDtypeStruct((8, LANES), f32)],
        compiler_params=pltpu.CompilerParams(vmem_limit_bytes=VMEM_LIMIT),
        cost_estimate=cost(16 * half * LANES, 10 * 4 * half * LANES),
    )(*parts_a, *parts_b)


def adam_update(gradient, master, first, second, clip_factor):
    scaled = clip_factor * gradient
    new_first = beta_first * first + (1.0 - beta_first) * scaled
    new_second = beta_second * second + (1.0 - beta_second) * scaled * scaled
    direction = new_first / correct_first / (jnp.sqrt(new_second / correct_second) + tiny_eps)
    new_master = master - learn_rate * (decay_rate * master + direction)
    return (new_master, new_first, new_second)


def clip_of(squares):
    total = jnp.sum(jnp.sum(squares[...], axis=0, keepdims=True), axis=1, keepdims=True)
    return jnp.minimum(1.0, clip_limit / (jnp.sqrt(total) + norm_eps))


def params_kernel(squares, *refs):
    clip_factor = clip_of(squares)
    for ins, out in ((refs[0:4], refs[8]), (refs[4:8], refs[9])):
        new_master, _, _ = adam_update(*(r[...] for r in ins), clip_factor)
        out[...] = new_master.astype(bf16)


def new_params(squares, means, states):
    half = means[0].shape[0]
    steps = half // BLOCK
    whole = pl.BlockSpec((8, LANES), lambda i: (0, 0))
    low = pl.BlockSpec((BLOCK, LANES), lambda i: (i, 0))
    high = pl.BlockSpec((BLOCK, LANES), lambda i: (steps + i, 0))
    return pl.pallas_call(
        params_kernel,
        grid=(steps,),
        in_specs=[whole, low, low, low, low, low, high, high, high],
        out_specs=[low, low],
        out_shape=[jax.ShapeDtypeStruct((half, LANES), bf16)] * 2,
        compiler_params=pltpu.CompilerParams(vmem_limit_bytes=VMEM_LIMIT),
        cost_estimate=cost(40 * half * LANES, 36 * half * LANES),
    )(squares, means[0], *states, means[1], *states)


def states_both_kernel(squares, mean_a, mean_b, master, first, second, *outs):
    clip_factor = clip_of(squares)
    for at, mean in enumerate((mean_a, mean_b)):
        values = adam_update(mean[...], master[at], first[at], second[at], clip_factor)
        for out, value in zip(outs, values):
            out[at] = value


def both_states(squares, means, states):
    half = means[0].shape[0]
    whole = pl.BlockSpec((8, LANES), lambda i: (0, 0))
    low = pl.BlockSpec((BLOCK, LANES), lambda i: (i, 0))
    pair = pl.BlockSpec((2, BLOCK, LANES), lambda i: (0, i, 0))
    return pl.pallas_call(
        states_both_kernel,
        grid=(half // BLOCK,),
        in_specs=[whole, low, low, pair, pair, pair],
        out_specs=[pair] * 3,
        out_shape=[jax.ShapeDtypeStruct((2, half, LANES), f32)] * 3,
        compiler_params=pltpu.CompilerParams(vmem_limit_bytes=VMEM_LIMIT),
        cost_estimate=cost(40 * half * LANES, 60 * half * LANES),
    )(squares, *means, *(s.reshape(2, half, LANES) for s in states))


def place_kernel(moves, n_parts, where, *refs):
    parts, out, sems = refs[:n_parts], refs[-2], refs[-1]
    copies = []
    for k, (source, target) in enumerate(moves):
        src = source(parts)
        dst = target(out, where)
        copies.append(pltpu.make_async_copy(src, dst, sems.at[k]))
    for copy in copies:
        copy.start()
    for copy in copies:
        copy.wait()


def place(out, where, parts, moves, shape):
    extra = [] if out is None else [out]
    any_ = pl.BlockSpec(memory_space=pl.ANY)
    return pl.pallas_call(
        functools.partial(place_kernel, moves, len(parts)),
        grid_spec=pltpu.PrefetchScalarGridSpec(
            num_scalar_prefetch=1,
            grid=(),
            in_specs=[any_] * (len(parts) + len(extra)),
            out_specs=any_,
            scratch_shapes=[pltpu.SemaphoreType.DMA((len(moves),))],
        ),
        out_shape=jax.ShapeDtypeStruct(shape, bf16),
        input_output_aliases={} if out is None else {len(parts) + 1: 0},
        compiler_params=pltpu.CompilerParams(vmem_limit_bytes=VMEM_LIMIT),
        cost_estimate=cost(0, 2 * sum(p.size for p in parts) * 2),
    )(where, *parts, *extra)


def shards(local_grads, master_weights, first_moment, second_moment):
    layers, flat = local_grads.shape[2:]
    rows = layers * flat // LANES // 16
    half = rows // 2
    z, x = lax.axis_index(Z), lax.axis_index(X)

    def to_rows(value):
        return value.reshape(layers, -1, LANES).transpose(1, 0, 2).reshape(-1, LANES)

    def from_rows(value):
        return value.reshape(-1, layers, LANES).transpose(1, 0, 2).reshape(1, layers, -1)

    pieces = to_rows(local_grads[0, 0]).reshape(4, 4, rows, LANES)
    states = [to_rows(s[0]) for s in (master_weights, first_moment, second_moment)]
    zx = jnp.stack([z, x]).astype(jnp.int32)
    xz = jnp.stack([x, z]).astype(jnp.int32)

    def for_z(by):
        at = lax.rem(z + by, 4)
        return lax.dynamic_slice(pieces, (at, 0, 0, 0), (1, 4, half, LANES)).reshape(4, half, LANES)

    def for_x(by):
        at = lax.rem(x + by, 4)
        return lax.dynamic_slice(pieces, (0, at, half, 0), (4, 1, half, LANES)).reshape(4, half, LANES)

    shifts = (1, 3, 2)
    got_z = [shift(for_z(s), Z, s) for s in shifts]
    got_x = [shift(for_x(s), X, s) for s in shifts]
    sums_a = first_sum(pieces, got_z, zx, True)
    sums_b = first_sum(pieces, got_x, xz, False)
    parts_a = [sums_a[0]] + [shift(sums_a[s], X, s) for s in shifts]
    parts_b = [sums_b[0]] + [shift(sums_b[s], Z, s) for s in shifts]
    mean_a, mean_b, squares = last_sum(parts_a, parts_b)

    for axis in (Z, X, Y):
        squares = squares + shift(squares, axis, 1) + shift(squares, axis, 3) + shift(squares, axis, 2)
    squares = squares + shift(squares, CORE, 1)

    par_a, par_b = new_params(squares, (mean_a, mean_b), states)
    outs = both_states(squares, (mean_a, mean_b), states)
    outs = [from_rows(o.reshape(rows, LANES)) for o in outs]

    def turn(i, by):
        return lax.rem(i + by, 4)

    row_a = [par_a] + [shift(par_a, X, s) for s in (1, 2, 3)]
    row_b = [par_b] + [shift(par_b, Z, s) for s in (1, 2, 3)]
    shape = (4, half, LANES)
    moves = [(lambda p, s=s: p[s], lambda o, w, s=s: o.at[turn(w[1], 4 - s)]) for s in range(4)]
    line_a = place(None, zx, row_a, moves, shape)
    line_b = place(None, xz, row_b, moves, shape)
    full = (4, 4, 2, half, LANES)

    def to_a(by, lo=0, n=half):
        return lambda o, w: o.at[turn(w[0], by), :, 0, pl.ds(lo, n)]

    def to_b(by, lo=0, n=half):
        return lambda o, w: o.at[:, turn(w[1], by), 1, pl.ds(lo, n)]

    out = place(None, zx, [line_a, line_b], [(lambda p: p[0], to_a(0)), (lambda p: p[1], to_b(0))], full)
    near = [shift(line_a, Z, 1), shift(line_a, Z, 3), shift(line_b, X, 1), shift(line_b, X, 3)]
    q = half // 2
    far = [
        shift(near[0][:, :q], Z, 1),
        shift(near[1][:, q:], Z, 3),
        shift(near[2][:, :q], X, 1),
        shift(near[3][:, q:], X, 3),
    ]
    out = place(
        out, zx, near,
        [(lambda p: p[0], to_a(3)), (lambda p: p[1], to_a(1)), (lambda p: p[2], to_b(3)), (lambda p: p[3], to_b(1))],
        full,
    )
    out = place(
        out, zx, far,
        [
            (lambda p: p[0], to_a(2, 0, q)),
            (lambda p: p[1], to_a(2, q, q)),
            (lambda p: p[2], to_b(2, 0, q)),
            (lambda p: p[3], to_b(2, q, q)),
        ],
        full,
    )
    return (from_rows(out.reshape(-1, LANES)), *outs)


def solution(mesh):
    torus = Mesh(mesh.devices.reshape(4, 4, 4, 2), (Z, X, Y, CORE))
    dp, expert = (Z, X), (Y, CORE)
    return jax.shard_map(
        shards,
        mesh=torus,
        in_specs=(P(dp, expert, None, None), P(expert, None, dp), P(expert, None, dp), P(expert, None, dp)),
        out_specs=(P(expert, None, None), P(expert, None, dp), P(expert, None, dp), P(expert, None, dp)),
        check_vma=False,
    )
```

```python
import functools

import jax
import jax.numpy as jnp
from jax import lax
from jax.experimental import pallas as pl
from jax.experimental.pallas import tpu as pltpu
from jax.sharding import Mesh
from jax.sharding import PartitionSpec as P

Z, X, Y, CORE = "z", "x", "y", "core"
beta_first = 0.9
beta_second = 0.95
correct_first = 1.0 - 0.9**10
correct_second = 1.0 - 0.95**10
learn_rate = 0.05
decay_rate = 0.1
clip_limit = 1.0
tiny_eps = 1e-08
norm_eps = 1e-06

LANES = 128
BLOCK = 256
VMEM_LIMIT = 12 * 2**20
f32, bf16 = jnp.float32, jnp.bfloat16


def shift(value, axis, by):
    size = lax.axis_size(axis)
    return lax.ppermute(value, axis, [(i, (i + by) % size) for i in range(size)])


def cost(flops, moved):
    return pl.CostEstimate(flops=flops, bytes_accessed=moved, transcendentals=0)


def pick_kernel(along_z, by, where, pieces, out, sems):
    quarter = out.shape[1] // 2
    low = 0 if along_z else 2 * quarter
    far_low = low if by == 1 else low + quarter
    near, far = lax.rem(where[0] + by, 4), lax.rem(where[0] + 2, 4)

    def source(at, start, count):
        rows = pl.ds(start, count)
        return pieces.at[at, :, rows] if along_z else pieces.at[:, at, rows]

    copies = [pltpu.make_async_copy(source(near, low, 2 * quarter), out.at[pl.ds(0, 4)], sems.at[0])]
    for j in range(4):
        rows = pl.ds(far_low, quarter)
        piece = pieces.at[far, j, rows] if along_z else pieces.at[j, far, rows]
        copies.append(pltpu.make_async_copy(piece, out.at[4 + j // 2, pl.ds(j % 2 * quarter, quarter)], sems.at[1 + j]))
    for copy in copies:
        copy.start()
    for copy in copies:
        copy.wait()


def pick(pieces, where, along_z, by):
    half = pieces.shape[2] // 2
    return pl.pallas_call(
        functools.partial(pick_kernel, along_z, by),
        grid_spec=pltpu.PrefetchScalarGridSpec(
            num_scalar_prefetch=1,
            grid=(),
            in_specs=[pl.BlockSpec(memory_space=pl.ANY)],
            out_specs=pl.BlockSpec(memory_space=pl.ANY),
            scratch_shapes=[pltpu.SemaphoreType.DMA((5,))],
        ),
        out_shape=jax.ShapeDtypeStruct((6, half, LANES), bf16),
        compiler_params=pltpu.CompilerParams(vmem_limit_bytes=VMEM_LIMIT),
        cost_estimate=cost(0, 24 * half * LANES),
    )(where, pieces)


def own_kernel(where, pieces, out_a, out_b, sems):
    half = out_a.shape[1]
    copies = [
        pltpu.make_async_copy(pieces.at[where[0], :, pl.ds(0, half)], out_a, sems.at[0]),
        pltpu.make_async_copy(pieces.at[:, where[1], pl.ds(half, half)], out_b, sems.at[1]),
    ]
    for copy in copies:
        copy.start()
    for copy in copies:
        copy.wait()


def own_pieces(pieces, zx):
    half = pieces.shape[2] // 2
    return pl.pallas_call(
        own_kernel,
        grid_spec=pltpu.PrefetchScalarGridSpec(
            num_scalar_prefetch=1,
            grid=(),
            in_specs=[pl.BlockSpec(memory_space=pl.ANY)],
            out_specs=[pl.BlockSpec(memory_space=pl.ANY)] * 2,
            scratch_shapes=[pltpu.SemaphoreType.DMA((2,))],
        ),
        out_shape=[jax.ShapeDtypeStruct((4, half, LANES), bf16)] * 2,
        compiler_params=pltpu.CompilerParams(vmem_limit_bytes=VMEM_LIMIT),
        cost_estimate=cost(0, 32 * half * LANES),
    )(zx, pieces)


def total_of(refs, at, far):
    own, behind, ahead = refs
    return own[at].astype(f32) + behind[at].astype(f32) + ahead[at].astype(f32) + far[at].astype(f32)


def far_sum_kernel(where, own, behind, ahead, far_low, far_high, low, high):
    at = lax.rem(where[1] + 2, 4)

    @pl.when(pl.program_id(0) < pl.num_programs(0) // 2)
    def _():
        low[...] = total_of((own, behind, ahead), at, far_low)

    @pl.when(pl.program_id(0) >= pl.num_programs(0) // 2)
    def _():
        high[...] = total_of((own, behind, ahead), at, far_high)


def near_sum_kernel(where, own, behind, ahead, far_low, far_high, *outs):
    def write(far):
        for by, out in zip((0, 1, 3), outs):
            out[...] = total_of((own, behind, ahead), lax.rem(where[1] + by, 4), far)

    pl.when(pl.program_id(0) < pl.num_programs(0) // 2)(lambda: write(far_low))
    pl.when(pl.program_id(0) >= pl.num_programs(0) // 2)(lambda: write(far_high))


def first_sum(where, own, behind, ahead, far_low, far_high, only_far):
    half = own.shape[1]
    quarter, steps = half // 2, half // BLOCK
    lower = lambda i: jnp.minimum(i, steps // 2 - 1)
    upper = lambda i: jnp.maximum(i - steps // 2, 0)
    part = pl.BlockSpec((4, BLOCK, LANES), lambda i, w: (0, i, 0))
    in_specs = [part] * 3 + [
        pl.BlockSpec((4, BLOCK, LANES), lambda i, w: (0, lower(i), 0)),
        pl.BlockSpec((4, BLOCK, LANES), lambda i, w: (0, upper(i), 0)),
    ]
    if only_far:
        out_specs = [
            pl.BlockSpec((BLOCK, LANES), lambda i, w: (lower(i), 0)),
            pl.BlockSpec((BLOCK, LANES), lambda i, w: (upper(i), 0)),
        ]
        out_shape = [jax.ShapeDtypeStruct((quarter, LANES), f32)] * 2
    else:
        out_specs = [pl.BlockSpec((BLOCK, LANES), lambda i, w: (i, 0))] * 3
        out_shape = [jax.ShapeDtypeStruct((half, LANES), f32)] * 3
    return pl.pallas_call(
        far_sum_kernel if only_far else near_sum_kernel,
        grid_spec=pltpu.PrefetchScalarGridSpec(
            num_scalar_prefetch=1, grid=(steps,), in_specs=in_specs, out_specs=out_specs
        ),
        out_shape=out_shape,
        compiler_params=pltpu.CompilerParams(vmem_limit_bytes=VMEM_LIMIT),
        cost_estimate=cost(16 * half * LANES, 4 * 4 * half * LANES * 3),
    )(where, own, behind, ahead, far_low.reshape(4, quarter, LANES), far_high.reshape(4, quarter, LANES))


def add_kernel(next_part, low, last_part, high, next_out, last_out):
    next_out[...] = next_part[...] + low[...]
    last_out[...] = last_part[...] + high[...]


def add_far(to_next, low, to_last, high):
    quarter = low.shape[0]
    steps = quarter // BLOCK
    first = pl.BlockSpec((BLOCK, LANES), lambda i: (i, 0))
    second = pl.BlockSpec((BLOCK, LANES), lambda i: (steps + i, 0))
    return pl.pallas_call(
        add_kernel,
        grid=(steps,),
        in_specs=[first, first, second, first],
        out_specs=[first, second],
        out_shape=[jax.ShapeDtypeStruct(to_next.shape, f32)] * 2,
        input_output_aliases={0: 0, 2: 1},
        compiler_params=pltpu.CompilerParams(vmem_limit_bytes=VMEM_LIMIT),
        cost_estimate=cost(2 * quarter * LANES, 24 * quarter * LANES),
    )(to_next, low, to_last, high)


def last_sum_kernel(*refs):
    parts_a, parts_b, (mean_a, mean_b, squares, held) = refs[:3], refs[3:6], refs[6:]

    @pl.when(pl.program_id(0) == 0)
    def _():
        held[...] = jnp.zeros_like(held)

    for parts, mean in ((parts_a, mean_a), (parts_b, mean_b)):
        total = (parts[0][...] + parts[1][...] + parts[2][...]) * (1.0 / 16.0)
        mean[...] = total
        held[...] += jnp.sum((total * total).reshape(BLOCK // 8, 8, LANES), axis=0)

    @pl.when(pl.program_id(0) == pl.num_programs(0) - 1)
    def _():
        squares[...] = jnp.broadcast_to(jnp.sum(held[...], axis=0, keepdims=True), squares.shape)


def last_sum(parts_a, parts_b, devices):
    half = parts_a[0].shape[0]
    block = pl.BlockSpec((BLOCK, LANES), lambda i: (i, 0))
    return pl.pallas_call(
        last_sum_kernel,
        grid=(half // BLOCK,),
        in_specs=[block] * 6,
        out_specs=[block, block, pl.BlockSpec((devices, LANES), lambda i: (0, 0))],
        out_shape=[jax.ShapeDtypeStruct((half, LANES), f32)] * 2 + [jax.ShapeDtypeStruct((devices, LANES), f32)],
        scratch_shapes=[pltpu.VMEM((8, LANES), f32)],
        compiler_params=pltpu.CompilerParams(vmem_limit_bytes=VMEM_LIMIT),
        cost_estimate=cost(16 * half * LANES, 10 * 4 * half * LANES),
    )(*parts_a, *parts_b)


def adam_update(gradient, master, first, second, clip_factor):
    scaled = clip_factor * gradient
    new_first = beta_first * first + (1.0 - beta_first) * scaled
    new_second = beta_second * second + (1.0 - beta_second) * scaled * scaled
    direction = new_first / correct_first / (jnp.sqrt(new_second / correct_second) + tiny_eps)
    new_master = master - learn_rate * (decay_rate * master + direction)
    return (new_master, new_first, new_second)


def clip_of(squares):
    total = jnp.sum(jnp.sum(squares[...], axis=0, keepdims=True), axis=1, keepdims=True)
    return jnp.minimum(1.0, clip_limit / (jnp.sqrt(total) + norm_eps))


def params_kernel(squares, *refs):
    clip_factor = clip_of(squares)
    for ins, out in ((refs[0:4], refs[8]), (refs[4:8], refs[9])):
        new_master, _, _ = adam_update(*(r[...] for r in ins), clip_factor)
        out[...] = new_master.astype(bf16)


def new_params(squares, means, states):
    half = means[0].shape[0]
    steps = half // BLOCK
    whole = pl.BlockSpec(squares.shape, lambda i: (0, 0))
    low = pl.BlockSpec((BLOCK, LANES), lambda i: (i, 0))
    high = pl.BlockSpec((BLOCK, LANES), lambda i: (steps + i, 0))
    return pl.pallas_call(
        params_kernel,
        grid=(steps,),
        in_specs=[whole, low, low, low, low, low, high, high, high],
        out_specs=[low, low],
        out_shape=[jax.ShapeDtypeStruct((half, LANES), bf16)] * 2,
        compiler_params=pltpu.CompilerParams(vmem_limit_bytes=VMEM_LIMIT),
        cost_estimate=cost(40 * half * LANES, 36 * half * LANES),
    )(squares, means[0], *states, means[1], *states)


def states_both_kernel(squares, mean_a, mean_b, master, first, second, *outs):
    clip_factor = clip_of(squares)
    for at, mean in enumerate((mean_a, mean_b)):
        values = adam_update(mean[...], master[at], first[at], second[at], clip_factor)
        for out, value in zip(outs, values):
            out[at] = value


def both_states(squares, means, states):
    half = means[0].shape[0]
    whole = pl.BlockSpec(squares.shape, lambda i: (0, 0))
    low = pl.BlockSpec((BLOCK, LANES), lambda i: (i, 0))
    pair = pl.BlockSpec((2, BLOCK, LANES), lambda i: (0, i, 0))
    return pl.pallas_call(
        states_both_kernel,
        grid=(half // BLOCK,),
        in_specs=[whole, low, low, pair, pair, pair],
        out_specs=[pair] * 3,
        out_shape=[jax.ShapeDtypeStruct((2, half, LANES), f32)] * 3,
        compiler_params=pltpu.CompilerParams(vmem_limit_bytes=VMEM_LIMIT),
        cost_estimate=cost(40 * half * LANES, 60 * half * LANES),
    )(squares, *means, *(s.reshape(2, half, LANES) for s in states))


def place_kernel(moves, n_parts, where, *refs):
    parts, out, sems = refs[:n_parts], refs[-2], refs[-1]
    copies = []
    for k, (source, target) in enumerate(moves):
        src = source(parts)
        dst = target(out, where)
        copies.append(pltpu.make_async_copy(src, dst, sems.at[k]))
    for copy in copies:
        copy.start()
    for copy in copies:
        copy.wait()


def place(out, where, parts, moves, shape):
    extra = [] if out is None else [out]
    any_ = pl.BlockSpec(memory_space=pl.ANY)
    return pl.pallas_call(
        functools.partial(place_kernel, moves, len(parts)),
        grid_spec=pltpu.PrefetchScalarGridSpec(
            num_scalar_prefetch=1,
            grid=(),
            in_specs=[any_] * (len(parts) + len(extra)),
            out_specs=any_,
            scratch_shapes=[pltpu.SemaphoreType.DMA((len(moves),))],
        ),
        out_shape=jax.ShapeDtypeStruct(shape, bf16),
        input_output_aliases={} if out is None else {len(parts) + 1: 0},
        compiler_params=pltpu.CompilerParams(vmem_limit_bytes=VMEM_LIMIT),
        cost_estimate=cost(0, 2 * sum(p.size for p in parts) * 2),
    )(where, *parts, *extra)


def shards(local_grads, master_weights, first_moment, second_moment):
    layers, flat = local_grads.shape[2:]
    rows = layers * flat // LANES // 16
    half = rows // 2
    z, x = lax.axis_index(Z), lax.axis_index(X)

    def to_rows(value):
        return value.reshape(layers, -1, LANES).transpose(1, 0, 2).reshape(-1, LANES)

    def from_rows(value):
        return value.reshape(-1, layers, LANES).transpose(1, 0, 2).reshape(1, layers, -1)

    pieces = to_rows(local_grads[0, 0]).reshape(4, 4, rows, LANES)
    states = [to_rows(s[0]) for s in (master_weights, first_moment, second_moment)]
    zx = jnp.stack([z, x]).astype(jnp.int32)
    xz = jnp.stack([x, z]).astype(jnp.int32)

    own_a, own_b = own_pieces(pieces, zx)
    sends = [pick(pieces, zx, True, 1), pick(pieces, zx, True, 3), pick(pieces, xz, False, 1), pick(pieces, xz, False, 3)]
    axes = (Z, Z, X, X)
    ways = (1, 3, 1, 3)
    got = [shift(v, axis, by) for v, axis, by in zip(sends, axes, ways)]
    far = [shift(v[4:], axis, by) for v, axis, by in zip(got, axes, ways)]
    set_a = (zx, own_a, got[0], got[1], far[0], far[1])
    set_b = (xz, own_b, got[2], got[3], far[2], far[3])
    low_a, high_a = first_sum(*set_a, True)
    low_b, high_b = first_sum(*set_b, True)
    low_a, high_a = shift(low_a, X, 1), shift(high_a, X, 3)
    low_b, high_b = shift(low_b, Z, 1), shift(high_b, Z, 3)
    here_a, next_a, last_a = first_sum(*set_a, False)
    here_b, next_b, last_b = first_sum(*set_b, False)
    next_a, last_a = add_far(next_a, low_a, last_a, high_a)
    next_b, last_b = add_far(next_b, low_b, last_b, high_b)
    parts_a = here_a, shift(next_a, X, 1), shift(last_a, X, 3)
    parts_b = here_b, shift(next_b, Z, 1), shift(last_b, Z, 3)
    devices = lax.axis_size((Z, X, Y, CORE))
    mean_a, mean_b, squares = last_sum(parts_a, parts_b, devices)
    squares = lax.all_to_all(squares, (Z, X, Y, CORE), 0, 0, tiled=True)

    par_a, par_b = new_params(squares, (mean_a, mean_b), states)
    outs = both_states(squares, (mean_a, mean_b), states)
    outs = [from_rows(o.reshape(rows, LANES)) for o in outs]

    def turn(i, by):
        return lax.rem(i + by, 4)

    row_a = [par_a] + [shift(par_a, X, s) for s in (1, 2, 3)]
    row_b = [par_b] + [shift(par_b, Z, s) for s in (1, 2, 3)]
    shape = (4, half, LANES)
    moves = [(lambda p, s=s: p[s], lambda o, w, s=s: o.at[turn(w[1], 4 - s)]) for s in range(4)]
    line_a = place(None, zx, row_a, moves, shape)
    line_b = place(None, xz, row_b, moves, shape)
    full = (4, 4, 2, half, LANES)

    def to_a(by, lo=0, n=half):
        return lambda o, w: o.at[turn(w[0], by), :, 0, pl.ds(lo, n)]

    def to_b(by, lo=0, n=half):
        return lambda o, w: o.at[:, turn(w[1], by), 1, pl.ds(lo, n)]

    out = place(None, zx, [line_a, line_b], [(lambda p: p[0], to_a(0)), (lambda p: p[1], to_b(0))], full)
    near = [shift(line_a, Z, 1), shift(line_a, Z, 3), shift(line_b, X, 1), shift(line_b, X, 3)]
    q = half // 2
    far = [
        shift(near[0][:, :q], Z, 1),
        shift(near[1][:, q:], Z, 3),
        shift(near[2][:, :q], X, 1),
        shift(near[3][:, q:], X, 3),
    ]
    out = place(
        out, zx, near,
        [(lambda p: p[0], to_a(3)), (lambda p: p[1], to_a(1)), (lambda p: p[2], to_b(3)), (lambda p: p[3], to_b(1))],
        full,
    )
    out = place(
        out, zx, far,
        [
            (lambda p: p[0], to_a(2, 0, q)),
            (lambda p: p[1], to_a(2, q, q)),
            (lambda p: p[2], to_b(2, 0, q)),
            (lambda p: p[3], to_b(2, q, q)),
        ],
        full,
    )
    return (from_rows(out.reshape(-1, LANES)), *outs)


def solution(mesh):
    torus = Mesh(mesh.devices.reshape(4, 4, 4, 2), (Z, X, Y, CORE))
    dp, expert = (Z, X), (Y, CORE)
    return jax.shard_map(
        shards,
        mesh=torus,
        in_specs=(P(dp, expert, None, None), P(expert, None, dp), P(expert, None, dp), P(expert, None, dp)),
        out_specs=(P(expert, None, None), P(expert, None, dp), P(expert, None, dp), P(expert, None, dp)),
        check_vma=False,
    )
```

```python
import functools

import jax
import jax.numpy as jnp
from jax import lax
from jax.experimental import pallas as pl
from jax.experimental.pallas import tpu as pltpu
from jax.sharding import Mesh
from jax.sharding import PartitionSpec as P

Z, X, Y, CORE = "z", "x", "y", "core"
beta_first = 0.9
beta_second = 0.95
correct_first = 1.0 - 0.9**10
correct_second = 1.0 - 0.95**10
learn_rate = 0.05
decay_rate = 0.1
clip_limit = 1.0
tiny_eps = 1e-08
norm_eps = 1e-06

LANES = 128
BLOCK = 256
VMEM_LIMIT = 12 * 2**20
f32, bf16 = jnp.float32, jnp.bfloat16


def shift(value, axis, by):
    size = lax.axis_size(axis)
    return lax.ppermute(value, axis, [(i, (i + by) % size) for i in range(size)])


def cost(flops, moved):
    return pl.CostEstimate(flops=flops, bytes_accessed=moved, transcendentals=0)


def pick_kernel(along_z, where, pieces, *refs):
    outs, sems = refs[:2], refs[2]
    quarter = outs[0].shape[1] // 2
    copies = []
    for k, (out, by) in enumerate(zip(outs, (1, 3))):
        me = where[0] if along_z else where[1]
        low = 0 if along_z else 2 * quarter
        far_low = low if by == 1 else low + quarter
        near, far = lax.rem(me + by, 4), lax.rem(me + 2, 4)
        rows = pl.ds(low, 2 * quarter)
        piece = pieces.at[near, :, rows] if along_z else pieces.at[:, near, rows]
        copies.append(pltpu.make_async_copy(piece, out.at[pl.ds(0, 4)], sems.at[k, 0]))
        for j in range(4):
            rows = pl.ds(far_low, quarter)
            piece = pieces.at[far, j, rows] if along_z else pieces.at[j, far, rows]
            target = out.at[4 + j // 2, pl.ds(j % 2 * quarter, quarter)]
            copies.append(pltpu.make_async_copy(piece, target, sems.at[k, 1 + j]))
    for copy in copies:
        copy.start()
    for copy in copies:
        copy.wait()


def pick(pieces, zx, along_z):
    half = pieces.shape[2] // 2
    return pl.pallas_call(
        functools.partial(pick_kernel, along_z),
        grid_spec=pltpu.PrefetchScalarGridSpec(
            num_scalar_prefetch=1,
            grid=(),
            in_specs=[pl.BlockSpec(memory_space=pl.ANY)],
            out_specs=[pl.BlockSpec(memory_space=pl.ANY)] * 2,
            scratch_shapes=[pltpu.SemaphoreType.DMA((2, 5))],
        ),
        out_shape=[jax.ShapeDtypeStruct((6, half, LANES), bf16)] * 2,
        compiler_params=pltpu.CompilerParams(vmem_limit_bytes=VMEM_LIMIT),
        cost_estimate=cost(0, 48 * half * LANES),
    )(zx, pltpu.with_memory_space_constraint(pieces, pltpu.HBM))


def own_kernel(where, pieces, out_a, out_b, sems):
    half = out_a.shape[1]
    copies = [
        pltpu.make_async_copy(pieces.at[where[0], :, pl.ds(0, half)], out_a, sems.at[0]),
        pltpu.make_async_copy(pieces.at[:, where[1], pl.ds(half, half)], out_b, sems.at[1]),
    ]
    for copy in copies:
        copy.start()
    for copy in copies:
        copy.wait()


def own_pieces(pieces, zx):
    half = pieces.shape[2] // 2
    return pl.pallas_call(
        own_kernel,
        grid_spec=pltpu.PrefetchScalarGridSpec(
            num_scalar_prefetch=1,
            grid=(),
            in_specs=[pl.BlockSpec(memory_space=pl.ANY)],
            out_specs=[pl.BlockSpec(memory_space=pl.ANY)] * 2,
            scratch_shapes=[pltpu.SemaphoreType.DMA((2,))],
        ),
        out_shape=[jax.ShapeDtypeStruct((4, half, LANES), bf16)] * 2,
        compiler_params=pltpu.CompilerParams(vmem_limit_bytes=VMEM_LIMIT),
        cost_estimate=cost(0, 32 * half * LANES),
    )(zx, pltpu.with_memory_space_constraint(pieces, pltpu.HBM))


def total_of(refs, at, far):
    own, behind, ahead = refs
    return own[at].astype(f32) + behind[at].astype(f32) + ahead[at].astype(f32) + far[at].astype(f32)


def far_sum_kernel(where, own, behind, ahead, far_low, far_high, low, high):
    at = lax.rem(where[1] + 2, 4)

    @pl.when(pl.program_id(0) < pl.num_programs(0) // 2)
    def _():
        low[...] = total_of((own, behind, ahead), at, far_low)

    @pl.when(pl.program_id(0) >= pl.num_programs(0) // 2)
    def _():
        high[...] = total_of((own, behind, ahead), at, far_high)


def near_sum_kernel(where, own, behind, ahead, far_low, far_high, *outs):
    def write(far):
        for by, out in zip((0, 1, 3), outs):
            out[...] = total_of((own, behind, ahead), lax.rem(where[1] + by, 4), far)

    pl.when(pl.program_id(0) < pl.num_programs(0) // 2)(lambda: write(far_low))
    pl.when(pl.program_id(0) >= pl.num_programs(0) // 2)(lambda: write(far_high))


def first_sum(where, own, behind, ahead, far_low, far_high, only_far):
    half = own.shape[1]
    quarter, steps = half // 2, half // BLOCK
    lower = lambda i: jnp.minimum(i, steps // 2 - 1)
    upper = lambda i: jnp.maximum(i - steps // 2, 0)
    part = pl.BlockSpec((4, BLOCK, LANES), lambda i, w: (0, i, 0))
    in_specs = [part] * 3 + [
        pl.BlockSpec((4, BLOCK, LANES), lambda i, w: (0, lower(i), 0)),
        pl.BlockSpec((4, BLOCK, LANES), lambda i, w: (0, upper(i), 0)),
    ]
    if only_far:
        out_specs = [
            pl.BlockSpec((BLOCK, LANES), lambda i, w: (lower(i), 0)),
            pl.BlockSpec((BLOCK, LANES), lambda i, w: (upper(i), 0)),
        ]
        out_shape = [jax.ShapeDtypeStruct((quarter, LANES), f32)] * 2
    else:
        out_specs = [pl.BlockSpec((BLOCK, LANES), lambda i, w: (i, 0))] * 3
        out_shape = [jax.ShapeDtypeStruct((half, LANES), f32)] * 3
    return pl.pallas_call(
        far_sum_kernel if only_far else near_sum_kernel,
        grid_spec=pltpu.PrefetchScalarGridSpec(
            num_scalar_prefetch=1, grid=(steps,), in_specs=in_specs, out_specs=out_specs
        ),
        out_shape=out_shape,
        compiler_params=pltpu.CompilerParams(vmem_limit_bytes=VMEM_LIMIT),
        cost_estimate=cost(16 * half * LANES, 4 * 4 * half * LANES * 3),
    )(where, own, behind, ahead, far_low.reshape(4, quarter, LANES), far_high.reshape(4, quarter, LANES))


def add_kernel(next_part, low, last_part, high, next_out, last_out):
    next_out[...] = next_part[...] + low[...]
    last_out[...] = last_part[...] + high[...]


def add_far(to_next, low, to_last, high):
    quarter = low.shape[0]
    steps = quarter // BLOCK
    first = pl.BlockSpec((BLOCK, LANES), lambda i: (i, 0))
    second = pl.BlockSpec((BLOCK, LANES), lambda i: (steps + i, 0))
    return pl.pallas_call(
        add_kernel,
        grid=(steps,),
        in_specs=[first, first, second, first],
        out_specs=[first, second],
        out_shape=[jax.ShapeDtypeStruct(to_next.shape, f32)] * 2,
        input_output_aliases={0: 0, 2: 1},
        compiler_params=pltpu.CompilerParams(vmem_limit_bytes=VMEM_LIMIT),
        cost_estimate=cost(2 * quarter * LANES, 24 * quarter * LANES),
    )(to_next, low, to_last, high)


def last_sum_kernel(*refs):
    parts_a, parts_b, (mean_a, mean_b, squares, held) = refs[:3], refs[3:6], refs[6:]

    @pl.when(pl.program_id(0) == 0)
    def _():
        held[...] = jnp.zeros_like(held)

    for parts, mean in ((parts_a, mean_a), (parts_b, mean_b)):
        total = (parts[0][...] + parts[1][...] + parts[2][...]) * (1.0 / 16.0)
        mean[...] = total
        held[...] += jnp.sum((total * total).reshape(BLOCK // 8, 8, LANES), axis=0)

    @pl.when(pl.program_id(0) == pl.num_programs(0) - 1)
    def _():
        squares[...] = jnp.broadcast_to(jnp.sum(held[...], axis=0, keepdims=True), squares.shape)


def last_sum(parts_a, parts_b, devices):
    half = parts_a[0].shape[0]
    block = pl.BlockSpec((BLOCK, LANES), lambda i: (i, 0))
    return pl.pallas_call(
        last_sum_kernel,
        grid=(half // BLOCK,),
        in_specs=[block] * 6,
        out_specs=[block, block, pl.BlockSpec((devices, LANES), lambda i: (0, 0))],
        out_shape=[jax.ShapeDtypeStruct((half, LANES), f32)] * 2 + [jax.ShapeDtypeStruct((devices, LANES), f32)],
        scratch_shapes=[pltpu.VMEM((8, LANES), f32)],
        compiler_params=pltpu.CompilerParams(vmem_limit_bytes=VMEM_LIMIT),
        cost_estimate=cost(16 * half * LANES, 10 * 4 * half * LANES),
    )(*parts_a, *parts_b)


def adam_update(gradient, master, first, second, clip_factor):
    scaled = clip_factor * gradient
    new_first = beta_first * first + (1.0 - beta_first) * scaled
    new_second = beta_second * second + (1.0 - beta_second) * scaled * scaled
    direction = new_first / correct_first / (jnp.sqrt(new_second / correct_second) + tiny_eps)
    new_master = master - learn_rate * (decay_rate * master + direction)
    return (new_master, new_first, new_second)


def clip_of(squares):
    total = jnp.sum(jnp.sum(squares[...], axis=0, keepdims=True), axis=1, keepdims=True)
    return jnp.minimum(1.0, clip_limit / (jnp.sqrt(total) + norm_eps))


def params_kernel(squares, mean_a, mean_b, master, first, second, *outs):
    clip_factor = clip_of(squares)
    for at, out in enumerate(outs):
        mean = (mean_a, mean_b)[at // 2]
        new_master, _, _ = adam_update(mean[at % 2], master[at], first[at], second[at], clip_factor)
        out[...] = new_master.astype(bf16)


def new_params(squares, means, states):
    quarter = means[0].shape[0] // 2
    whole = pl.BlockSpec(squares.shape, lambda i: (0, 0))
    two = pl.BlockSpec((2, BLOCK, LANES), lambda i: (0, i, 0))
    four = pl.BlockSpec((4, BLOCK, LANES), lambda i: (0, i, 0))
    return pl.pallas_call(
        params_kernel,
        grid=(quarter // BLOCK,),
        in_specs=[whole, two, two, four, four, four],
        out_specs=[pl.BlockSpec((BLOCK, LANES), lambda i: (i, 0))] * 4,
        out_shape=[jax.ShapeDtypeStruct((quarter, LANES), bf16)] * 4,
        compiler_params=pltpu.CompilerParams(vmem_limit_bytes=VMEM_LIMIT),
        cost_estimate=cost(160 * quarter * LANES, 72 * quarter * LANES),
    )(
        squares,
        *(m.reshape(2, quarter, LANES) for m in means),
        *(s.reshape(4, quarter, LANES) for s in states),
    )


def states_both_kernel(squares, mean_a, mean_b, master, first, second, *outs):
    clip_factor = clip_of(squares)
    for at, mean in enumerate((mean_a, mean_b)):
        values = adam_update(mean[...], master[at], first[at], second[at], clip_factor)
        for out, value in zip(outs, values):
            out[at] = value


def both_states(squares, means, states):
    half = means[0].shape[0]
    whole = pl.BlockSpec(squares.shape, lambda i: (0, 0))
    low = pl.BlockSpec((BLOCK, LANES), lambda i: (i, 0))
    pair = pl.BlockSpec((2, BLOCK, LANES), lambda i: (0, i, 0))
    return pl.pallas_call(
        states_both_kernel,
        grid=(half // BLOCK,),
        in_specs=[whole, low, low, pair, pair, pair],
        out_specs=[pair] * 3,
        out_shape=[jax.ShapeDtypeStruct((2, half, LANES), f32)] * 3,
        compiler_params=pltpu.CompilerParams(vmem_limit_bytes=VMEM_LIMIT),
        cost_estimate=cost(40 * half * LANES, 60 * half * LANES),
    )(squares, *means, *(s.reshape(2, half, LANES) for s in states))


DIMS = {"zA": (Z, 1), "zB": (Z, 3), "xA": (X, 1), "xB": (X, 3)}
ORDERS = (("zA", "xA", "zB", "xB"), ("xA", "zB", "xB", "zA"), ("zB", "xB", "zA", "xA"), ("xB", "zA", "xA", "zB"))


def partner(value, dim):
    axis, mask = DIMS[dim]
    return lax.ppermute(value, axis, [(i, i ^ mask) for i in range(4)])


def join_kernel(one, two, out, sems):
    size = one.shape[0]
    copies = [
        pltpu.make_async_copy(one, out.at[pl.ds(0, size)], sems.at[0]),
        pltpu.make_async_copy(two, out.at[pl.ds(size, size)], sems.at[1]),
    ]
    for copy in copies:
        copy.start()
    for copy in copies:
        copy.wait()


def join(one, two):
    any_ = pl.BlockSpec(memory_space=pl.ANY)
    return pl.pallas_call(
        join_kernel,
        in_specs=[any_, any_],
        out_specs=any_,
        scratch_shapes=[pltpu.SemaphoreType.DMA((2,))],
        out_shape=jax.ShapeDtypeStruct((2 * one.shape[0],) + one.shape[1:], one.dtype),
        compiler_params=pltpu.CompilerParams(vmem_limit_bytes=VMEM_LIMIT),
        cost_estimate=cost(0, 4 * one.size),
    )(one, two)


def masks_of(order):
    found = [(0, 0)]
    for dim in order:
        axis, mask = DIMS[dim]
        found += [(mz ^ mask, mx) if axis == Z else (mz, mx ^ mask) for mz, mx in found]
    return found


def set_kernel(jobs, n_parts, *refs):
    parts, out, sems = refs[:n_parts], refs[-2], refs[-1]
    z, x = lax.axis_index(Z), lax.axis_index(X)
    copies = []
    for k, (part, entry, chain, mz, mx) in enumerate(jobs):
        target = out.at[lax.bitwise_xor(z, mz), lax.bitwise_xor(x, mx), chain]
        copies.append(pltpu.make_async_copy(parts[part].at[entry], target, sems.at[k]))
    for copy in copies:
        copy.start()
    for copy in copies:
        copy.wait()


def set_blocks(out, parts, jobs, shape):
    extra = [] if out is None else [out]
    any_ = pl.BlockSpec(memory_space=pl.ANY)
    return pl.pallas_call(
        functools.partial(set_kernel, jobs, len(parts)),
        in_specs=[any_] * (len(parts) + len(extra)),
        out_specs=any_,
        scratch_shapes=[pltpu.SemaphoreType.DMA((len(jobs),))],
        out_shape=jax.ShapeDtypeStruct(shape, bf16),
        input_output_aliases={} if out is None else {len(parts): 0},
        compiler_params=pltpu.CompilerParams(vmem_limit_bytes=VMEM_LIMIT),
        cost_estimate=cost(0, 4 * sum(p.size for p in parts)),
    )(*parts, *extra)


def gather_blocks(blocks):
    held = [b[None] for b in blocks]
    for step in range(3):
        sent = [partner(h, order[step]) for h, order in zip(held, ORDERS)]
        held = [join(h, s) for h, s in zip(held, sent)]
    sent = [partner(h, order[3]) for h, order in zip(held, ORDERS)]
    shape = (4, 4, 4) + blocks[0].shape
    masks = [masks_of(order) for order in ORDERS]
    out = set_blocks(None, held, [(c, e, c) + masks[c][e] for c in range(4) for e in range(8)], shape)
    for c in range(4):
        out = set_blocks(out, [sent[c]], [(0, e, c) + masks[c][8 + e] for e in range(8)], shape)
    return out


def shards(local_grads, master_weights, first_moment, second_moment):
    layers, flat = local_grads.shape[2:]
    rows = layers * flat // LANES // 16
    half = rows // 2
    z, x = lax.axis_index(Z), lax.axis_index(X)

    def to_rows(value):
        return value.reshape(layers, -1, LANES).transpose(1, 0, 2).reshape(-1, LANES)

    def from_rows(value):
        return value.reshape(-1, layers, LANES).transpose(1, 0, 2).reshape(1, layers, -1)

    pieces = to_rows(local_grads[0, 0]).reshape(4, 4, rows, LANES)
    states = [to_rows(s[0]) for s in (master_weights, first_moment, second_moment)]
    zx = jnp.stack([z, x]).astype(jnp.int32)
    xz = jnp.stack([x, z]).astype(jnp.int32)

    own_a, own_b = own_pieces(pieces, zx)
    sends = pick(pieces, zx, True) + pick(pieces, zx, False)
    axes = (Z, Z, X, X)
    ways = (1, 3, 1, 3)
    got = [shift(v, axis, by) for v, axis, by in zip(sends, axes, ways)]
    far = [shift(v[4:], axis, by) for v, axis, by in zip(got, axes, ways)]
    set_a = (zx, own_a, got[0], got[1], far[0], far[1])
    set_b = (xz, own_b, got[2], got[3], far[2], far[3])
    low_a, high_a = first_sum(*set_a, True)
    low_b, high_b = first_sum(*set_b, True)
    low_a, high_a = shift(low_a, X, 1), shift(high_a, X, 3)
    low_b, high_b = shift(low_b, Z, 1), shift(high_b, Z, 3)
    here_a, next_a, last_a = first_sum(*set_a, False)
    here_b, next_b, last_b = first_sum(*set_b, False)
    next_a, last_a = add_far(next_a, low_a, last_a, high_a)
    next_b, last_b = add_far(next_b, low_b, last_b, high_b)
    parts_a = here_a, shift(next_a, X, 1), shift(last_a, X, 3)
    parts_b = here_b, shift(next_b, Z, 1), shift(last_b, Z, 3)
    devices = lax.axis_size((Z, X, Y, CORE))
    mean_a, mean_b, squares = last_sum(parts_a, parts_b, devices)
    squares = lax.all_to_all(squares, (Z, X, Y, CORE), 0, 0, tiled=True)

    blocks = new_params(squares, (mean_a, mean_b), states)
    outs = both_states(squares, (mean_a, mean_b), states)
    outs = [from_rows(o.reshape(rows, LANES)) for o in outs]
    out = gather_blocks(blocks)
    return (from_rows(out.reshape(-1, LANES)), *outs)


def solution(mesh):
    torus = Mesh(mesh.devices.reshape(4, 4, 4, 2), (Z, X, Y, CORE))
    dp, expert = (Z, X), (Y, CORE)
    return jax.shard_map(
        shards,
        mesh=torus,
        in_specs=(P(dp, expert, None, None), P(expert, None, dp), P(expert, None, dp), P(expert, None, dp)),
        out_specs=(P(expert, None, None), P(expert, None, dp), P(expert, None, dp), P(expert, None, dp)),
        check_vma=False,
    )
```

```python
import functools

import jax
import jax.numpy as jnp
from jax import lax
from jax.experimental import pallas as pl
from jax.experimental.pallas import tpu as pltpu
from jax.sharding import Mesh
from jax.sharding import PartitionSpec as P

Z, X, Y, CORE = "z", "x", "y", "core"
beta_first = 0.9
beta_second = 0.95
correct_first = 1.0 - 0.9**10
correct_second = 1.0 - 0.95**10
learn_rate = 0.05
decay_rate = 0.1
clip_limit = 1.0
tiny_eps = 1e-08
norm_eps = 1e-06

LANES = 128
BLOCK = 256
VMEM_LIMIT = 12 * 2**20
f32, bf16 = jnp.float32, jnp.bfloat16


def shift(value, axis, by):
    size = lax.axis_size(axis)
    return lax.ppermute(value, axis, [(i, (i + by) % size) for i in range(size)])


def cost(flops, moved):
    return pl.CostEstimate(flops=flops, bytes_accessed=moved, transcendentals=0)


def pick_kernel(at_z, at_x, pieces, *refs):
    outs, sems = refs[:4], refs[4]
    quarter = outs[0].shape[1] // 2
    z, x = at_z[0], at_x[0]
    copies = []
    for k, (out, along_z, by) in enumerate(zip(outs, (True, True, False, False), (1, 3, 1, 3))):
        me = z if along_z else x
        low = 0 if along_z else 2 * quarter
        far_low = low if by == 1 else low + quarter
        near, far = lax.rem(me + by, 4), lax.rem(me + 2, 4)
        rows = pl.ds(low, 2 * quarter)
        piece = pieces.at[near, :, rows] if along_z else pieces.at[:, near, rows]
        copies.append(pltpu.make_async_copy(piece, out.at[pl.ds(0, 4)], sems.at[k, 0]))
        for j in range(4):
            rows = pl.ds(far_low, quarter)
            piece = pieces.at[far, j, rows] if along_z else pieces.at[j, far, rows]
            target = out.at[4 + j // 2, pl.ds(j % 2 * quarter, quarter)]
            copies.append(pltpu.make_async_copy(piece, target, sems.at[k, 1 + j]))
    for copy in copies:
        copy.start()
    for copy in copies:
        copy.wait()


def pick(pieces, z, x):
    half = pieces.shape[2] // 2
    any_ = pl.BlockSpec(memory_space=pl.ANY)
    return pl.pallas_call(
        pick_kernel,
        grid_spec=pltpu.PrefetchScalarGridSpec(
            num_scalar_prefetch=2,
            grid=(),
            in_specs=[any_],
            out_specs=[any_] * 4,
            scratch_shapes=[pltpu.SemaphoreType.DMA((4, 5))],
        ),
        out_shape=[jax.ShapeDtypeStruct((6, half, LANES), bf16)] * 4,
        compiler_params=pltpu.CompilerParams(vmem_limit_bytes=VMEM_LIMIT),
        cost_estimate=cost(0, 96 * half * LANES),
    )(z.reshape(1), x.reshape(1), pltpu.with_memory_space_constraint(pieces, pltpu.HBM))


def base_kernel(where, own, behind, ahead, out):
    out[...] = own[...].astype(f32) + behind[...].astype(f32) + ahead[...].astype(f32)


def base_sum(where, pieces, behind, ahead, along_z):
    half = behind.shape[1]
    steps = half // BLOCK
    part = pl.BlockSpec((4, BLOCK, LANES), lambda i, w: (0, i, 0))
    if along_z:
        own = pl.BlockSpec((None, 4, BLOCK, LANES), lambda i, w: (w[0], 0, i, 0))
    else:
        own = pl.BlockSpec((4, None, BLOCK, LANES), lambda i, w: (0, w[0], steps + i, 0))
    return pl.pallas_call(
        base_kernel,
        grid_spec=pltpu.PrefetchScalarGridSpec(
            num_scalar_prefetch=1, grid=(steps,), in_specs=[own, part, part], out_specs=part
        ),
        out_shape=jax.ShapeDtypeStruct((4, half, LANES), f32),
        compiler_params=pltpu.CompilerParams(vmem_limit_bytes=VMEM_LIMIT),
        cost_estimate=cost(8 * half * LANES, 40 * half * LANES),
    )(where, pltpu.with_memory_space_constraint(pieces, pltpu.HBM), behind, ahead)


def on_half(low_part, high_part):
    pl.when(pl.program_id(0) < pl.num_programs(0) // 2)(low_part)
    pl.when(pl.program_id(0) >= pl.num_programs(0) // 2)(high_part)


def far_sum_kernel(where, base, far_low, far_high, low, high):
    def low_part():
        low[...] = base[...] + far_low[...].astype(f32)

    def high_part():
        high[...] = base[...] + far_high[...].astype(f32)

    on_half(low_part, high_part)


def far_sum(where, base, far_low, far_high):
    quarter = far_low.shape[1]
    out = pl.BlockSpec((quarter, LANES), lambda i, w: (0, 0))
    far = pl.BlockSpec((None, quarter, LANES), lambda i, w: (lax.rem(w[1] + 2, 4), 0, 0))
    return pl.pallas_call(
        far_sum_kernel,
        grid_spec=pltpu.PrefetchScalarGridSpec(
            num_scalar_prefetch=1,
            grid=(2,),
            in_specs=[pl.BlockSpec((None, quarter, LANES), lambda i, w: (lax.rem(w[1] + 2, 4), i, 0)), far, far],
            out_specs=[out, out],
        ),
        out_shape=[jax.ShapeDtypeStruct((quarter, LANES), f32)] * 2,
        compiler_params=pltpu.CompilerParams(vmem_limit_bytes=VMEM_LIMIT),
        cost_estimate=cost(2 * quarter * LANES, 20 * quarter * LANES),
    )(where, base, far_low, far_high)


def near_sum_kernel(where, base_1, base_3, low_1, low_3, high_1, high_3, came_low, came_high, to_next, to_last):
    def low_part():
        to_next[...] = base_1[...] + low_1[...].astype(f32) + came_low[...]
        to_last[...] = base_3[...] + low_3[...].astype(f32)

    def high_part():
        to_next[...] = base_1[...] + high_1[...].astype(f32)
        to_last[...] = base_3[...] + high_3[...].astype(f32) + came_high[...]

    on_half(low_part, high_part)


def near_sum(where, base, far_low, far_high, came_low, came_high):
    quarter = far_low.shape[1]
    whole = pl.BlockSpec((quarter, LANES), lambda i, w: (0, 0))
    out = pl.BlockSpec((quarter, LANES), lambda i, w: (i, 0))

    def base_at(by):
        return pl.BlockSpec((None, quarter, LANES), lambda i, w: (lax.rem(w[1] + by, 4), i, 0))

    def far_at(by):
        return pl.BlockSpec((None, quarter, LANES), lambda i, w: (lax.rem(w[1] + by, 4), 0, 0))

    return pl.pallas_call(
        near_sum_kernel,
        grid_spec=pltpu.PrefetchScalarGridSpec(
            num_scalar_prefetch=1,
            grid=(2,),
            in_specs=[base_at(1), base_at(3), far_at(1), far_at(3), far_at(1), far_at(3), whole, whole],
            out_specs=[out, out],
        ),
        out_shape=[jax.ShapeDtypeStruct((2 * quarter, LANES), f32)] * 2,
        compiler_params=pltpu.CompilerParams(vmem_limit_bytes=VMEM_LIMIT),
        cost_estimate=cost(10 * quarter * LANES, 48 * quarter * LANES),
    )(where, base, base, far_low, far_low, far_high, far_high, came_low, came_high)


def here_sum_kernel(zx, *refs):
    sets, outs = (refs[:3], refs[3:6]), refs[6:]

    def add(which):
        for parts, out in zip(sets, outs):
            out[...] = parts[0][...] + parts[which][...].astype(f32)

    on_half(lambda: add(1), lambda: add(2))


def here_sum(zx, base_a, low_a, high_a, base_b, low_b, high_b):
    quarter = low_a.shape[1]

    def set_specs(at):
        far = pl.BlockSpec((None, quarter, LANES), lambda i, w: (w[at], 0, 0))
        return [pl.BlockSpec((None, quarter, LANES), lambda i, w: (w[at], i, 0)), far, far]

    return pl.pallas_call(
        here_sum_kernel,
        grid_spec=pltpu.PrefetchScalarGridSpec(
            num_scalar_prefetch=1,
            grid=(2,),
            in_specs=set_specs(1) + set_specs(0),
            out_specs=[pl.BlockSpec((quarter, LANES), lambda i, w: (i, 0))] * 2,
        ),
        out_shape=[jax.ShapeDtypeStruct((2 * quarter, LANES), f32)] * 2,
        compiler_params=pltpu.CompilerParams(vmem_limit_bytes=VMEM_LIMIT),
        cost_estimate=cost(4 * quarter * LANES, 40 * quarter * LANES),
    )(zx, base_a, low_a, high_a, base_b, low_b, high_b)


def last_sum_kernel(*refs):
    parts_a, parts_b, (mean_a, mean_b, squares, held) = refs[:3], refs[3:6], refs[6:]

    @pl.when(pl.program_id(0) == 0)
    def _():
        held[...] = jnp.zeros_like(held)

    for parts, mean in ((parts_a, mean_a), (parts_b, mean_b)):
        total = (parts[0][...] + parts[1][...] + parts[2][...]) * (1.0 / 16.0)
        mean[...] = total
        held[...] += jnp.sum((total * total).reshape(BLOCK // 8, 8, LANES), axis=0)

    @pl.when(pl.program_id(0) == pl.num_programs(0) - 1)
    def _():
        squares[...] = jnp.broadcast_to(jnp.sum(held[...], axis=0, keepdims=True), squares.shape)


def last_sum(parts_a, parts_b, devices):
    half = parts_a[0].shape[0]
    block = pl.BlockSpec((BLOCK, LANES), lambda i: (i, 0))
    return pl.pallas_call(
        last_sum_kernel,
        grid=(half // BLOCK,),
        in_specs=[block] * 6,
        out_specs=[block, block, pl.BlockSpec((devices, LANES), lambda i: (0, 0))],
        out_shape=[jax.ShapeDtypeStruct((half, LANES), f32)] * 2 + [jax.ShapeDtypeStruct((devices, LANES), f32)],
        scratch_shapes=[pltpu.VMEM((8, LANES), f32)],
        compiler_params=pltpu.CompilerParams(vmem_limit_bytes=VMEM_LIMIT),
        cost_estimate=cost(16 * half * LANES, 10 * 4 * half * LANES),
    )(*parts_a, *parts_b)


def adam_update(gradient, master, first, second, clip_factor):
    scaled = clip_factor * gradient
    new_first = beta_first * first + (1.0 - beta_first) * scaled
    new_second = beta_second * second + (1.0 - beta_second) * scaled * scaled
    direction = (new_first * (1.0 / correct_first)) / (jnp.sqrt(new_second * (1.0 / correct_second)) + tiny_eps)
    new_master = master - learn_rate * (decay_rate * master + direction)
    return (new_master, new_first, new_second)


def clip_of(squares):
    total = jnp.sum(jnp.sum(squares[...], axis=0, keepdims=True), axis=1, keepdims=True)
    return jnp.minimum(1.0, clip_limit / (jnp.sqrt(total) + norm_eps))


def params_kernel(squares, mean_a, mean_b, master, first, second, *outs):
    clip_factor = clip_of(squares)
    for at, out in enumerate(outs):
        mean = (mean_a, mean_b)[at // 2]
        new_master, _, _ = adam_update(mean[at % 2], master[at], first[at], second[at], clip_factor)
        out[...] = new_master.astype(bf16)


def new_params(squares, means, states):
    quarter = means[0].shape[0] // 2
    whole = pl.BlockSpec(squares.shape, lambda i: (0, 0))
    two = pl.BlockSpec((2, BLOCK, LANES), lambda i: (0, i, 0))
    four = pl.BlockSpec((4, BLOCK, LANES), lambda i: (0, i, 0))
    return pl.pallas_call(
        params_kernel,
        grid=(quarter // BLOCK,),
        in_specs=[whole, two, two, four, four, four],
        out_specs=[pl.BlockSpec((BLOCK, LANES), lambda i: (i, 0))] * 4,
        out_shape=[jax.ShapeDtypeStruct((quarter, LANES), bf16)] * 4,
        compiler_params=pltpu.CompilerParams(vmem_limit_bytes=VMEM_LIMIT),
        cost_estimate=cost(160 * quarter * LANES, 72 * quarter * LANES),
    )(
        squares,
        *(m.reshape(2, quarter, LANES) for m in means),
        *(s.reshape(4, quarter, LANES) for s in states),
    )


def states_both_kernel(squares, mean_a, mean_b, master, first, second, *outs):
    clip_factor = clip_of(squares)
    for at, mean in enumerate((mean_a, mean_b)):
        values = adam_update(mean[...], master[at], first[at], second[at], clip_factor)
        for out, value in zip(outs, values):
            out[at] = value


def both_states(squares, means, states):
    half = means[0].shape[0]
    whole = pl.BlockSpec(squares.shape, lambda i: (0, 0))
    low = pl.BlockSpec((BLOCK, LANES), lambda i: (i, 0))
    pair = pl.BlockSpec((2, BLOCK, LANES), lambda i: (0, i, 0))
    return pl.pallas_call(
        states_both_kernel,
        grid=(half // BLOCK,),
        in_specs=[whole, low, low, pair, pair, pair],
        out_specs=[pair] * 3,
        out_shape=[jax.ShapeDtypeStruct((2, half, LANES), f32)] * 3,
        compiler_params=pltpu.CompilerParams(vmem_limit_bytes=VMEM_LIMIT),
        cost_estimate=cost(40 * half * LANES, 60 * half * LANES),
    )(squares, *means, *(s.reshape(2, half, LANES) for s in states))


DIMS = {"zA": (Z, 1), "zB": (Z, 3), "xA": (X, 1), "xB": (X, 3)}
ORDERS = (("zA", "xA", "zB", "xB"), ("xA", "zB", "xB", "zA"), ("zB", "xB", "zA", "xA"), ("xB", "zA", "xA", "zB"))


def partner(value, dim):
    axis, mask = DIMS[dim]
    return lax.ppermute(value, axis, [(i, i ^ mask) for i in range(4)])


def join_kernel(one, two, out, sems):
    size = one.shape[0]
    copies = [
        pltpu.make_async_copy(one, out.at[pl.ds(0, size)], sems.at[0]),
        pltpu.make_async_copy(two, out.at[pl.ds(size, size)], sems.at[1]),
    ]
    for copy in copies:
        copy.start()
    for copy in copies:
        copy.wait()


def join(one, two):
    any_ = pl.BlockSpec(memory_space=pl.ANY)
    return pl.pallas_call(
        join_kernel,
        in_specs=[any_, any_],
        out_specs=any_,
        scratch_shapes=[pltpu.SemaphoreType.DMA((2,))],
        out_shape=jax.ShapeDtypeStruct((2 * one.shape[0],) + one.shape[1:], one.dtype),
        compiler_params=pltpu.CompilerParams(vmem_limit_bytes=VMEM_LIMIT),
        cost_estimate=cost(0, 4 * one.size),
    )(one, two)


def masks_of(order):
    found = [(0, 0)]
    for dim in order:
        axis, mask = DIMS[dim]
        found += [(mz ^ mask, mx) if axis == Z else (mz, mx ^ mask) for mz, mx in found]
    return found


def set_kernel(jobs, n_parts, *refs):
    parts, out, sems = refs[:n_parts], refs[-2], refs[-1]
    z, x = lax.axis_index(Z), lax.axis_index(X)
    copies = []
    for k, (part, entry, chain, mz, mx) in enumerate(jobs):
        target = out.at[lax.bitwise_xor(z, mz), lax.bitwise_xor(x, mx), chain]
        copies.append(pltpu.make_async_copy(parts[part].at[entry], target, sems.at[k]))
    for copy in copies:
        copy.start()
    for copy in copies:
        copy.wait()


def set_blocks(out, parts, jobs, shape):
    extra = [] if out is None else [out]
    any_ = pl.BlockSpec(memory_space=pl.ANY)
    return pl.pallas_call(
        functools.partial(set_kernel, jobs, len(parts)),
        in_specs=[any_] * (len(parts) + len(extra)),
        out_specs=any_,
        scratch_shapes=[pltpu.SemaphoreType.DMA((len(jobs),))],
        out_shape=jax.ShapeDtypeStruct(shape, bf16),
        input_output_aliases={} if out is None else {len(parts): 0},
        compiler_params=pltpu.CompilerParams(vmem_limit_bytes=VMEM_LIMIT),
        cost_estimate=cost(0, 4 * sum(p.size for p in parts)),
    )(*parts, *extra)


def gather_blocks(blocks):
    held = [b[None] for b in blocks]
    for step in range(3):
        sent = [partner(h, order[step]) for h, order in zip(held, ORDERS)]
        held = [join(h, s) for h, s in zip(held, sent)]
    sent = [partner(h, order[3]) for h, order in zip(held, ORDERS)]
    shape = (4, 4, 4) + blocks[0].shape
    masks = [masks_of(order) for order in ORDERS]
    out = set_blocks(None, held, [(c, e, c) + masks[c][e] for c in range(4) for e in range(8)], shape)
    for c in range(4):
        out = set_blocks(out, [sent[c]], [(0, e, c) + masks[c][8 + e] for e in range(8)], shape)
    return out


def shards(local_grads, master_weights, first_moment, second_moment):
    layers, flat = local_grads.shape[2:]
    rows = layers * flat // LANES // 16
    half = rows // 2
    z, x = lax.axis_index(Z), lax.axis_index(X)

    def to_rows(value):
        return value.reshape(layers, -1, LANES).transpose(1, 0, 2).reshape(-1, LANES)

    def from_rows(value):
        return value.reshape(-1, layers, LANES).transpose(1, 0, 2).reshape(1, layers, -1)

    pieces = to_rows(local_grads[0, 0]).reshape(4, 4, rows, LANES)
    states = [to_rows(s[0]) for s in (master_weights, first_moment, second_moment)]
    zx = jnp.stack([z, x]).astype(jnp.int32)
    xz = jnp.stack([x, z]).astype(jnp.int32)

    sends = pick(pieces, z, x)
    axes = (Z, Z, X, X)
    ways = (1, 3, 1, 3)
    got = [shift(v, axis, by) for v, axis, by in zip(sends, axes, ways)]
    far = [shift(v[4:], axis, by).reshape(4, half // 2, LANES) for v, axis, by in zip(got, axes, ways)]
    base_a = base_sum(zx, pieces, got[0], got[1], True)
    base_b = base_sum(xz, pieces, got[2], got[3], False)
    low_a, high_a = far_sum(zx, base_a, far[0], far[1])
    low_b, high_b = far_sum(xz, base_b, far[2], far[3])
    low_a, high_a = shift(low_a, X, 1), shift(high_a, X, 3)
    low_b, high_b = shift(low_b, Z, 1), shift(high_b, Z, 3)
    next_a, last_a = near_sum(zx, base_a, far[0], far[1], low_a, high_a)
    next_b, last_b = near_sum(xz, base_b, far[2], far[3], low_b, high_b)
    here_a, here_b = here_sum(zx, base_a, far[0], far[1], base_b, far[2], far[3])
    parts_a = here_a, shift(next_a, X, 1), shift(last_a, X, 3)
    parts_b = here_b, shift(next_b, Z, 1), shift(last_b, Z, 3)
    devices = lax.axis_size((Z, X, Y, CORE))
    mean_a, mean_b, squares = last_sum(parts_a, parts_b, devices)
    squares = lax.all_to_all(squares, (Z, X, Y, CORE), 0, 0, tiled=True)

    blocks = new_params(squares, (mean_a, mean_b), states)
    outs = both_states(squares, (mean_a, mean_b), states)
    outs = [from_rows(o.reshape(rows, LANES)) for o in outs]
    out = gather_blocks(blocks)
    return (from_rows(out.reshape(-1, LANES)), *outs)


def solution(mesh):
    torus = Mesh(mesh.devices.reshape(4, 4, 4, 2), (Z, X, Y, CORE))
    dp, expert = (Z, X), (Y, CORE)
    return jax.shard_map(
        shards,
        mesh=torus,
        in_specs=(P(dp, expert, None, None), P(expert, None, dp), P(expert, None, dp), P(expert, None, dp)),
        out_specs=(P(expert, None, None), P(expert, None, dp), P(expert, None, dp), P(expert, None, dp)),
        check_vma=False,
    )
```

```python
import functools

import jax
import jax.numpy as jnp
from jax import lax
from jax.experimental import pallas as pl
from jax.experimental.pallas import tpu as pltpu
from jax.sharding import Mesh
from jax.sharding import PartitionSpec as P

Z, X, Y, CORE = "z", "x", "y", "core"
beta_first = 0.9
beta_second = 0.95
correct_first = 1.0 - 0.9**10
correct_second = 1.0 - 0.95**10
learn_rate = 0.05
decay_rate = 0.1
clip_limit = 1.0
tiny_eps = 1e-08
norm_eps = 1e-06

LANES = 128
BLOCK = 256
CHUNK = 64
VMEM_LIMIT = 12 * 2**20
f32, bf16 = jnp.float32, jnp.bfloat16


def shift(value, axis, by):
    size = lax.axis_size(axis)
    return lax.ppermute(value, axis, [(i, (i + by) % size) for i in range(size)])


def cost(flops, moved):
    return pl.CostEstimate(flops=flops, bytes_accessed=moved, transcendentals=0)


def pick_kernel(at_z, at_x, pieces, *refs):
    outs, sems = refs[:4], refs[4]
    quarter = outs[0].shape[1] // 2
    z, x = at_z[0], at_x[0]
    copies = []
    for k, (out, along_z, by) in enumerate(zip(outs, (True, True, False, False), (1, 3, 1, 3))):
        me = z if along_z else x
        low = 0 if along_z else 2 * quarter
        far_low = low if by == 1 else low + quarter
        near, far = lax.rem(me + by, 4), lax.rem(me + 2, 4)
        rows = pl.ds(low, 2 * quarter)
        piece = pieces.at[near, :, rows] if along_z else pieces.at[:, near, rows]
        copies.append(pltpu.make_async_copy(piece, out.at[pl.ds(0, 4)], sems.at[k, 0]))
        for j in range(4):
            rows = pl.ds(far_low, quarter)
            piece = pieces.at[far, j, rows] if along_z else pieces.at[j, far, rows]
            target = out.at[4 + j // 2, pl.ds(j % 2 * quarter, quarter)]
            copies.append(pltpu.make_async_copy(piece, target, sems.at[k, 1 + j]))
    for copy in copies:
        copy.start()
    for copy in copies:
        copy.wait()


def pick(pieces, z, x):
    half = pieces.shape[2] // 2
    any_ = pl.BlockSpec(memory_space=pl.ANY)
    return pl.pallas_call(
        pick_kernel,
        grid_spec=pltpu.PrefetchScalarGridSpec(
            num_scalar_prefetch=2,
            grid=(),
            in_specs=[any_],
            out_specs=[any_] * 4,
            scratch_shapes=[pltpu.SemaphoreType.DMA((4, 5))],
        ),
        out_shape=[jax.ShapeDtypeStruct((6, half, LANES), bf16)] * 4,
        compiler_params=pltpu.CompilerParams(vmem_limit_bytes=VMEM_LIMIT),
        cost_estimate=cost(0, 96 * half * LANES),
    )(z.reshape(1), x.reshape(1), pltpu.with_memory_space_constraint(pieces, pltpu.HBM))


def base_kernel(where, own, behind, ahead, out):
    out[...] = own[...].astype(f32) + behind[...].astype(f32) + ahead[...].astype(f32)


def base_sum(where, pieces, behind, ahead, along_z):
    half = behind.shape[1]
    steps = half // BLOCK
    part = pl.BlockSpec((4, BLOCK, LANES), lambda i, w: (0, i, 0))
    if along_z:
        own = pl.BlockSpec((None, 4, BLOCK, LANES), lambda i, w: (w[0], 0, i, 0))
    else:
        own = pl.BlockSpec((4, None, BLOCK, LANES), lambda i, w: (0, w[0], steps + i, 0))
    return pl.pallas_call(
        base_kernel,
        grid_spec=pltpu.PrefetchScalarGridSpec(
            num_scalar_prefetch=1, grid=(steps,), in_specs=[own, part, part], out_specs=part
        ),
        out_shape=jax.ShapeDtypeStruct((4, half, LANES), f32),
        compiler_params=pltpu.CompilerParams(vmem_limit_bytes=VMEM_LIMIT),
        cost_estimate=cost(8 * half * LANES, 40 * half * LANES),
    )(where, pltpu.with_memory_space_constraint(pieces, pltpu.HBM), behind, ahead)


def chunks_of(size):
    def run(body):
        @pl.loop(0, size // CHUNK)
        def _(i):
            body(pl.multiple_of(i * CHUNK, CHUNK))

    return run


def far_sum_kernel(axis, base, far_low, far_high, low, high):
    quarter = low.shape[0]
    at = lax.rem(lax.axis_index(axis) + 2, 4)

    @chunks_of(quarter)
    def _(start):
        rows, upper = pl.ds(start, CHUNK), pl.ds(quarter + start, CHUNK)
        low[rows] = base[at, rows] + far_low[at, rows].astype(f32)
        high[rows] = base[at, upper] + far_high[at, rows].astype(f32)


def far_sum(axis, base, far_low, far_high):
    quarter = far_low.shape[1]
    here = pl.BlockSpec(memory_space=pltpu.VMEM)
    return pl.pallas_call(
        functools.partial(far_sum_kernel, axis),
        in_specs=[here] * 3,
        out_specs=[here] * 2,
        out_shape=[jax.ShapeDtypeStruct((quarter, LANES), f32)] * 2,
        compiler_params=pltpu.CompilerParams(vmem_limit_bytes=VMEM_LIMIT),
        cost_estimate=cost(2 * quarter * LANES, 20 * quarter * LANES),
    )(base, far_low, far_high)


def near_sum_kernel(axis, base, far_low, far_high, came_low, came_high, to_next, to_last):
    quarter = came_low.shape[0]
    after = lax.rem(lax.axis_index(axis) + 1, 4)
    before = lax.rem(lax.axis_index(axis) + 3, 4)

    @chunks_of(quarter)
    def _(start):
        rows, upper = pl.ds(start, CHUNK), pl.ds(quarter + start, CHUNK)
        to_next[rows] = base[after, rows] + far_low[after, rows].astype(f32) + came_low[rows]
        to_next[upper] = base[after, upper] + far_high[after, rows].astype(f32)
        to_last[rows] = base[before, rows] + far_low[before, rows].astype(f32)
        to_last[upper] = base[before, upper] + far_high[before, rows].astype(f32) + came_high[rows]


def near_sum(axis, base, far_low, far_high, came_low, came_high):
    quarter = far_low.shape[1]
    here = pl.BlockSpec(memory_space=pltpu.VMEM)
    return pl.pallas_call(
        functools.partial(near_sum_kernel, axis),
        in_specs=[here] * 5,
        out_specs=[here] * 2,
        out_shape=[jax.ShapeDtypeStruct((2 * quarter, LANES), f32)] * 2,
        compiler_params=pltpu.CompilerParams(vmem_limit_bytes=VMEM_LIMIT),
        cost_estimate=cost(10 * quarter * LANES, 48 * quarter * LANES),
    )(base, far_low, far_high, came_low, came_high)


def here_sum_kernel(*refs):
    for axis, (base, far_low, far_high), out in zip((X, Z), (refs[:3], refs[3:6]), refs[6:]):
        quarter = far_low.shape[1]
        at = lax.axis_index(axis)

        @chunks_of(quarter)
        def _(start):
            rows, upper = pl.ds(start, CHUNK), pl.ds(quarter + start, CHUNK)
            out[rows] = base[at, rows] + far_low[at, rows].astype(f32)
            out[upper] = base[at, upper] + far_high[at, rows].astype(f32)


def here_sum(base_a, low_a, high_a, base_b, low_b, high_b):
    quarter = low_a.shape[1]
    here = pl.BlockSpec(memory_space=pltpu.VMEM)
    return pl.pallas_call(
        here_sum_kernel,
        in_specs=[here] * 6,
        out_specs=[here] * 2,
        out_shape=[jax.ShapeDtypeStruct((2 * quarter, LANES), f32)] * 2,
        compiler_params=pltpu.CompilerParams(vmem_limit_bytes=VMEM_LIMIT),
        cost_estimate=cost(4 * quarter * LANES, 40 * quarter * LANES),
    )(base_a, low_a, high_a, base_b, low_b, high_b)


def last_sum_kernel(*refs):
    parts_a, parts_b, (mean_a, mean_b, squares, held) = refs[:3], refs[3:6], refs[6:]
    held[...] = jnp.zeros_like(held)

    @chunks_of(mean_a.shape[0])
    def _(start):
        rows = pl.ds(start, CHUNK)
        for parts, mean in ((parts_a, mean_a), (parts_b, mean_b)):
            total = (parts[0][rows] + parts[1][rows] + parts[2][rows]) * (1.0 / 16.0)
            mean[rows] = total
            held[...] += jnp.sum((total * total).reshape(CHUNK // 8, 8, LANES), axis=0)

    squares[...] = jnp.broadcast_to(jnp.sum(held[...], axis=0, keepdims=True), squares.shape)


def last_sum(parts_a, parts_b, devices):
    half = parts_a[0].shape[0]
    here = pl.BlockSpec(memory_space=pltpu.VMEM)
    return pl.pallas_call(
        last_sum_kernel,
        in_specs=[here] * 6,
        out_specs=[here] * 3,
        out_shape=[jax.ShapeDtypeStruct((half, LANES), f32)] * 2 + [jax.ShapeDtypeStruct((devices, LANES), f32)],
        scratch_shapes=[pltpu.VMEM((8, LANES), f32)],
        compiler_params=pltpu.CompilerParams(vmem_limit_bytes=VMEM_LIMIT),
        cost_estimate=cost(16 * half * LANES, 10 * 4 * half * LANES),
    )(*parts_a, *parts_b)


def adam_update(gradient, master, first, second, clip_factor):
    scaled = clip_factor * gradient
    new_first = beta_first * first + (1.0 - beta_first) * scaled
    new_second = beta_second * second + (1.0 - beta_second) * scaled * scaled
    direction = (new_first * (1.0 / correct_first)) / (jnp.sqrt(new_second * (1.0 / correct_second)) + tiny_eps)
    new_master = master - learn_rate * (decay_rate * master + direction)
    return (new_master, new_first, new_second)


def clip_of(squares):
    total = jnp.sum(jnp.sum(squares[...], axis=0, keepdims=True), axis=1, keepdims=True)
    return jnp.minimum(1.0, clip_limit / (jnp.sqrt(total) + norm_eps))


def params_kernel(squares, mean_a, mean_b, master, first, second, *outs):
    clip_factor = clip_of(squares)
    quarter = outs[0].shape[0]
    for at, out in enumerate(outs):
        mean = (mean_a, mean_b)[at // 2]

        @pl.loop(0, quarter // CHUNK)
        def _(i):
            rows = pl.ds(pl.multiple_of(at * quarter + i * CHUNK, CHUNK), CHUNK)
            mean_rows = pl.ds(pl.multiple_of(at % 2 * quarter + i * CHUNK, CHUNK), CHUNK)
            new_master, _, _ = adam_update(mean[mean_rows], master[rows], first[rows], second[rows], clip_factor)
            out[pl.ds(pl.multiple_of(i * CHUNK, CHUNK), CHUNK)] = new_master.astype(bf16)


def new_params(squares, means, states):
    quarter = means[0].shape[0] // 2
    here = pl.BlockSpec(memory_space=pltpu.VMEM)
    operands = [value for value in (squares, *means, *states)]
    return pl.pallas_call(
        params_kernel,
        in_specs=[here] * 6,
        out_specs=[here] * 4,
        out_shape=[jax.ShapeDtypeStruct((quarter, LANES), bf16)] * 4,
        compiler_params=pltpu.CompilerParams(vmem_limit_bytes=VMEM_LIMIT),
        cost_estimate=cost(160 * quarter * LANES, 72 * quarter * LANES),
    )(*operands)


def states_both_kernel(squares, mean_a, mean_b, master, first, second, *outs):
    clip_factor = clip_of(squares)
    for at, mean in enumerate((mean_a, mean_b)):
        values = adam_update(mean[...], master[at], first[at], second[at], clip_factor)
        for out, value in zip(outs, values):
            out[at] = value


def both_states(squares, means, states):
    half = means[0].shape[0]
    whole = pl.BlockSpec(squares.shape, lambda i: (0, 0))
    low = pl.BlockSpec((BLOCK, LANES), lambda i: (i, 0))
    pair = pl.BlockSpec((2, BLOCK, LANES), lambda i: (0, i, 0))
    return pl.pallas_call(
        states_both_kernel,
        grid=(half // BLOCK,),
        in_specs=[whole, low, low, pair, pair, pair],
        out_specs=[pair] * 3,
        out_shape=[jax.ShapeDtypeStruct((2, half, LANES), f32)] * 3,
        compiler_params=pltpu.CompilerParams(vmem_limit_bytes=VMEM_LIMIT),
        cost_estimate=cost(40 * half * LANES, 60 * half * LANES),
    )(squares, *means, *(s.reshape(2, half, LANES) for s in states))


DIMS = {"zA": (Z, 1), "zB": (Z, 3), "xA": (X, 1), "xB": (X, 3)}
ORDERS = (("zA", "xA", "zB", "xB"), ("xA", "zB", "xB", "zA"), ("zB", "xB", "zA", "xA"), ("xB", "zA", "xA", "zB"))


def partner(value, dim):
    axis, mask = DIMS[dim]
    return lax.ppermute(value, axis, [(i, i ^ mask) for i in range(4)])


def join_kernel(one, two, out):
    size = one.shape[0]
    for i in range(size):
        out[i] = one[i]
        out[size + i] = two[i]


def join(one, two):
    here = pl.BlockSpec(memory_space=pltpu.VMEM)
    return pl.pallas_call(
        join_kernel,
        in_specs=[here, here],
        out_specs=here,
        out_shape=jax.ShapeDtypeStruct((2 * one.shape[0],) + one.shape[1:], one.dtype),
        compiler_params=pltpu.CompilerParams(vmem_limit_bytes=VMEM_LIMIT),
        cost_estimate=cost(0, 4 * one.size),
    )(one, two)


def masks_of(order):
    found = [(0, 0)]
    for dim in order:
        axis, mask = DIMS[dim]
        found += [(mz ^ mask, mx) if axis == Z else (mz, mx ^ mask) for mz, mx in found]
    return found


def set_kernel(jobs, n_parts, *refs):
    parts, out, sems = refs[:n_parts], refs[-2], refs[-1]
    z, x = lax.axis_index(Z), lax.axis_index(X)
    copies = []
    for k, (part, entry, chain, mz, mx) in enumerate(jobs):
        target = out.at[lax.bitwise_xor(z, mz), lax.bitwise_xor(x, mx), chain]
        copies.append(pltpu.make_async_copy(parts[part].at[entry], target, sems.at[k]))
    for copy in copies:
        copy.start()
    for copy in copies:
        copy.wait()


def set_blocks(out, parts, jobs, shape):
    extra = [] if out is None else [out]
    any_ = pl.BlockSpec(memory_space=pl.ANY)
    return pl.pallas_call(
        functools.partial(set_kernel, jobs, len(parts)),
        in_specs=[any_] * (len(parts) + len(extra)),
        out_specs=any_,
        scratch_shapes=[pltpu.SemaphoreType.DMA((len(jobs),))],
        out_shape=jax.ShapeDtypeStruct(shape, bf16),
        input_output_aliases={} if out is None else {len(parts): 0},
        compiler_params=pltpu.CompilerParams(vmem_limit_bytes=VMEM_LIMIT),
        cost_estimate=cost(0, 4 * sum(p.size for p in parts)),
    )(*parts, *extra)


def gather_blocks(blocks):
    held = [b[None] for b in blocks]
    for step in range(3):
        sent = [partner(h, order[step]) for h, order in zip(held, ORDERS)]
        held = [join(h, s) for h, s in zip(held, sent)]
    sent = [partner(h, order[3]) for h, order in zip(held, ORDERS)]
    shape = (4, 4, 4) + blocks[0].shape
    masks = [masks_of(order) for order in ORDERS]
    out = set_blocks(None, held, [(c, e, c) + masks[c][e] for c in range(4) for e in range(8)], shape)
    for c in range(4):
        out = set_blocks(out, [sent[c]], [(0, e, c) + masks[c][8 + e] for e in range(8)], shape)
    return out


def shards(local_grads, master_weights, first_moment, second_moment):
    layers, flat = local_grads.shape[2:]
    rows = layers * flat // LANES // 16
    half = rows // 2
    z, x = lax.axis_index(Z), lax.axis_index(X)

    def to_rows(value):
        return value.reshape(layers, -1, LANES).transpose(1, 0, 2).reshape(-1, LANES)

    def from_rows(value):
        return value.reshape(-1, layers, LANES).transpose(1, 0, 2).reshape(1, layers, -1)

    pieces = to_rows(local_grads[0, 0]).reshape(4, 4, rows, LANES)
    states = [to_rows(s[0]) for s in (master_weights, first_moment, second_moment)]
    zx = jnp.stack([z, x]).astype(jnp.int32)
    xz = jnp.stack([x, z]).astype(jnp.int32)

    sends = pick(pieces, z, x)
    axes = (Z, Z, X, X)
    ways = (1, 3, 1, 3)
    got = [shift(v, axis, by) for v, axis, by in zip(sends, axes, ways)]
    far = [shift(v[4:], axis, by).reshape(4, half // 2, LANES) for v, axis, by in zip(got, axes, ways)]
    base_a = base_sum(zx, pieces, got[0], got[1], True)
    base_b = base_sum(xz, pieces, got[2], got[3], False)
    low_a, high_a = far_sum(X, base_a, far[0], far[1])
    low_b, high_b = far_sum(Z, base_b, far[2], far[3])
    low_a, high_a = shift(low_a, X, 1), shift(high_a, X, 3)
    low_b, high_b = shift(low_b, Z, 1), shift(high_b, Z, 3)
    next_a, last_a = near_sum(X, base_a, far[0], far[1], low_a, high_a)
    next_b, last_b = near_sum(Z, base_b, far[2], far[3], low_b, high_b)
    here_a, here_b = here_sum(base_a, far[0], far[1], base_b, far[2], far[3])
    parts_a = here_a, shift(next_a, X, 1), shift(last_a, X, 3)
    parts_b = here_b, shift(next_b, Z, 1), shift(last_b, Z, 3)
    devices = lax.axis_size((Z, X, Y, CORE))
    mean_a, mean_b, squares = last_sum(parts_a, parts_b, devices)
    squares = lax.all_to_all(squares, (Z, X, Y, CORE), 0, 0, tiled=True)

    blocks = new_params(squares, (mean_a, mean_b), states)
    outs = both_states(squares, (mean_a, mean_b), states)
    outs = [from_rows(o.reshape(rows, LANES)) for o in outs]
    out = gather_blocks(blocks)
    return (from_rows(out.reshape(-1, LANES)), *outs)


def solution(mesh):
    torus = Mesh(mesh.devices.reshape(4, 4, 4, 2), (Z, X, Y, CORE))
    dp, expert = (Z, X), (Y, CORE)
    return jax.shard_map(
        shards,
        mesh=torus,
        in_specs=(P(dp, expert, None, None), P(expert, None, dp), P(expert, None, dp), P(expert, None, dp)),
        out_specs=(P(expert, None, None), P(expert, None, dp), P(expert, None, dp), P(expert, None, dp)),
        check_vma=False,
    )
```

```python
import functools

import jax
import jax.numpy as jnp
from jax import lax
from jax.experimental import pallas as pl
from jax.experimental.pallas import tpu as pltpu
from jax.sharding import Mesh
from jax.sharding import PartitionSpec as P

Z, X, Y, CORE = "z", "x", "y", "core"
beta_first = 0.9
beta_second = 0.95
correct_first = 1.0 - 0.9**10
correct_second = 1.0 - 0.95**10
learn_rate = 0.05
decay_rate = 0.1
clip_limit = 1.0
tiny_eps = 1e-08
norm_eps = 1e-06

LANES = 128
BLOCK = 256
VMEM_LIMIT = 12 * 2**20
f32, bf16 = jnp.float32, jnp.bfloat16


def shift(value, axis, by):
    size = lax.axis_size(axis)
    return lax.ppermute(value, axis, [(i, (i + by) % size) for i in range(size)])


def cost(flops, moved):
    return pl.CostEstimate(flops=flops, bytes_accessed=moved, transcendentals=0)


def pick_kernel(at_z, at_x, pieces, *refs):
    outs, sems = refs[:4], refs[4]
    z, x = at_z[0], at_x[0]
    half_a = outs[0].shape[1]
    copies = []
    for k, (out, along_z, by) in enumerate(zip(outs, (True, True, False, False), (1, 3, 1, 3))):
        half = out.shape[1]
        quarter = half // 2
        me = z if along_z else x
        low = 0 if along_z else half_a
        far_low = low if by == 1 else low + quarter
        near, far = lax.rem(me + by, 4), lax.rem(me + 2, 4)
        rows = pl.ds(low, half)
        piece = pieces.at[near, :, rows] if along_z else pieces.at[:, near, rows]
        copies.append(pltpu.make_async_copy(piece, out.at[pl.ds(0, 4)], sems.at[k, 0]))
        for j in range(4):
            rows = pl.ds(far_low, quarter)
            piece = pieces.at[far, j, rows] if along_z else pieces.at[j, far, rows]
            target = out.at[4 + j // 2, pl.ds(j % 2 * quarter, quarter)]
            copies.append(pltpu.make_async_copy(piece, target, sems.at[k, 1 + j]))
    for copy in copies:
        copy.start()
    for copy in copies:
        copy.wait()


def pick(pieces, z, x, halves):
    any_ = pl.BlockSpec(memory_space=pl.ANY)
    return pl.pallas_call(
        pick_kernel,
        grid_spec=pltpu.PrefetchScalarGridSpec(
            num_scalar_prefetch=2,
            grid=(),
            in_specs=[any_],
            out_specs=[any_] * 4,
            scratch_shapes=[pltpu.SemaphoreType.DMA((4, 5))],
        ),
        out_shape=[jax.ShapeDtypeStruct((6, half, LANES), bf16) for half in halves for _ in range(2)],
        compiler_params=pltpu.CompilerParams(vmem_limit_bytes=VMEM_LIMIT),
        cost_estimate=cost(0, 48 * sum(halves) * LANES),
    )(z.reshape(1), x.reshape(1), pltpu.with_memory_space_constraint(pieces, pltpu.HBM))


def own_kernel(pieces, out_a, out_b, sems):
    half_a, half_b = out_a.shape[1], out_b.shape[1]
    z, x = lax.axis_index(Z), lax.axis_index(X)
    copies = [
        pltpu.make_async_copy(pieces.at[z, :, pl.ds(0, half_a)], out_a, sems.at[0]),
        pltpu.make_async_copy(pieces.at[:, x, pl.ds(half_a, half_b)], out_b, sems.at[1]),
    ]
    for copy in copies:
        copy.start()
    for copy in copies:
        copy.wait()


def own_pieces(pieces, halves):
    any_ = pl.BlockSpec(memory_space=pl.ANY)
    return pl.pallas_call(
        own_kernel,
        in_specs=[any_],
        out_specs=[any_] * 2,
        scratch_shapes=[pltpu.SemaphoreType.DMA((2,))],
        out_shape=[jax.ShapeDtypeStruct((4, half, LANES), bf16) for half in halves],
        compiler_params=pltpu.CompilerParams(vmem_limit_bytes=VMEM_LIMIT),
        cost_estimate=cost(0, 16 * sum(halves) * LANES),
    )(pltpu.with_memory_space_constraint(pieces, pltpu.HBM))


def base_kernel(own, behind, ahead, out):
    for j in range(4):

        @chunks_of(out.shape[1])
        def _(rows):
            out[j, rows] = own[j, rows].astype(f32) + behind[j, rows].astype(f32) + ahead[j, rows].astype(f32)


def base_sum(own, behind, ahead):
    here = pl.BlockSpec(memory_space=pltpu.VMEM)
    return pl.pallas_call(
        base_kernel,
        in_specs=[here] * 3,
        out_specs=here,
        out_shape=jax.ShapeDtypeStruct(own.shape, f32),
        compiler_params=pltpu.CompilerParams(vmem_limit_bytes=VMEM_LIMIT),
        cost_estimate=cost(2 * own.size, 60 * own.size),
    )(own, behind, ahead)


def chunks_of(size, *starts):
    step = max(n for n in (64, 48, 32, 16) if size % n == 0)

    def run(body):
        @pl.loop(0, size // step)
        def _(i):
            body(*(pl.ds(pl.multiple_of(at + i * step, 16), step) for at in (0, *starts)))

    return run


def far_sum_kernel(axis, base, far_low, far_high, low, high):
    quarter = low.shape[0]
    at = lax.rem(lax.axis_index(axis) + 2, 4)

    @chunks_of(quarter, quarter)
    def _(rows, upper):
        low[rows] = base[at, rows] + far_low[at, rows].astype(f32)
        high[rows] = base[at, upper] + far_high[at, rows].astype(f32)


def far_sum(axis, base, far_low, far_high):
    quarter = far_low.shape[1]
    here = pl.BlockSpec(memory_space=pltpu.VMEM)
    return pl.pallas_call(
        functools.partial(far_sum_kernel, axis),
        in_specs=[here] * 3,
        out_specs=[here] * 2,
        out_shape=[jax.ShapeDtypeStruct((quarter, LANES), f32)] * 2,
        compiler_params=pltpu.CompilerParams(vmem_limit_bytes=VMEM_LIMIT),
        cost_estimate=cost(2 * quarter * LANES, 20 * quarter * LANES),
    )(base, far_low, far_high)


def near_sum_kernel(axis, base, far_low, far_high, came_low, came_high, to_next, to_last):
    quarter = came_low.shape[0]
    after = lax.rem(lax.axis_index(axis) + 1, 4)
    before = lax.rem(lax.axis_index(axis) + 3, 4)

    @chunks_of(quarter, quarter)
    def _(rows, upper):
        to_next[rows] = base[after, rows] + far_low[after, rows].astype(f32) + came_low[rows]
        to_next[upper] = base[after, upper] + far_high[after, rows].astype(f32)
        to_last[rows] = base[before, rows] + far_low[before, rows].astype(f32)
        to_last[upper] = base[before, upper] + far_high[before, rows].astype(f32) + came_high[rows]


def near_sum(axis, base, far_low, far_high, came_low, came_high):
    quarter = far_low.shape[1]
    here = pl.BlockSpec(memory_space=pltpu.VMEM)
    return pl.pallas_call(
        functools.partial(near_sum_kernel, axis),
        in_specs=[here] * 5,
        out_specs=[here] * 2,
        out_shape=[jax.ShapeDtypeStruct((2 * quarter, LANES), f32)] * 2,
        compiler_params=pltpu.CompilerParams(vmem_limit_bytes=VMEM_LIMIT),
        cost_estimate=cost(10 * quarter * LANES, 48 * quarter * LANES),
    )(base, far_low, far_high, came_low, came_high)


def here_sum_kernel(*refs):
    for axis, (base, far_low, far_high), out in zip((X, Z), (refs[:3], refs[3:6]), refs[6:]):
        quarter = far_low.shape[1]
        at = lax.axis_index(axis)

        @chunks_of(quarter, quarter)
        def _(rows, upper):
            out[rows] = base[at, rows] + far_low[at, rows].astype(f32)
            out[upper] = base[at, upper] + far_high[at, rows].astype(f32)


def here_sum(base_a, low_a, high_a, base_b, low_b, high_b):
    here = pl.BlockSpec(memory_space=pltpu.VMEM)
    return pl.pallas_call(
        here_sum_kernel,
        in_specs=[here] * 6,
        out_specs=[here] * 2,
        out_shape=[jax.ShapeDtypeStruct(base.shape[1:], f32) for base in (base_a, base_b)],
        compiler_params=pltpu.CompilerParams(vmem_limit_bytes=VMEM_LIMIT),
        cost_estimate=cost(base_a.size // 2, 5 * base_a.size),
    )(base_a, low_a, high_a, base_b, low_b, high_b)


def last_sum_kernel(*refs):
    parts_a, parts_b, (mean, squares, held) = refs[:3], refs[3:6], refs[6:]
    held[...] = jnp.zeros_like(held)
    for parts, first in ((parts_a, 0), (parts_b, parts_a[0].shape[0])):

        @chunks_of(parts[0].shape[0], first)
        def _(rows, target):
            total = (parts[0][rows] + parts[1][rows] + parts[2][rows]) * (1.0 / 16.0)
            mean[target] = total
            held[...] += jnp.sum((total * total).reshape(-1, 8, LANES), axis=0)

    squares[...] = jnp.broadcast_to(jnp.sum(held[...], axis=0, keepdims=True), squares.shape)


def last_sum(parts_a, parts_b, devices):
    rows = parts_a[0].shape[0] + parts_b[0].shape[0]
    here = pl.BlockSpec(memory_space=pltpu.VMEM)
    return pl.pallas_call(
        last_sum_kernel,
        in_specs=[here] * 6,
        out_specs=[here] * 2,
        out_shape=[jax.ShapeDtypeStruct((rows, LANES), f32), jax.ShapeDtypeStruct((devices, LANES), f32)],
        scratch_shapes=[pltpu.VMEM((8, LANES), f32)],
        compiler_params=pltpu.CompilerParams(vmem_limit_bytes=VMEM_LIMIT),
        cost_estimate=cost(8 * rows * LANES, 20 * rows * LANES),
    )(*parts_a, *parts_b)


def adam_update(gradient, master, first, second, clip_factor):
    scaled = clip_factor * gradient
    new_first = beta_first * first + (1.0 - beta_first) * scaled
    new_second = beta_second * second + (1.0 - beta_second) * scaled * scaled
    direction = (new_first * (1.0 / correct_first)) / (jnp.sqrt(new_second * (1.0 / correct_second)) + tiny_eps)
    new_master = master - learn_rate * (decay_rate * master + direction)
    return (new_master, new_first, new_second)


def clip_of(squares):
    total = jnp.sum(jnp.sum(squares[...], axis=0, keepdims=True), axis=1, keepdims=True)
    return jnp.minimum(1.0, clip_limit / (jnp.sqrt(total) + norm_eps))


def params_kernel(squares, mean, master, first, second, *outs):
    clip_factor = clip_of(squares)
    size = outs[0].shape[0]
    for at, out in enumerate(outs):

        @chunks_of(size, at * size)
        def _(target, rows):
            new_master, _, _ = adam_update(mean[rows], master[rows], first[rows], second[rows], clip_factor)
            out[target] = new_master.astype(bf16)


def new_params(squares, mean, states):
    quarter = mean.shape[0] // 4
    here = pl.BlockSpec(memory_space=pltpu.VMEM)
    return pl.pallas_call(
        params_kernel,
        in_specs=[here] * 5,
        out_specs=[here] * 4,
        out_shape=[jax.ShapeDtypeStruct((quarter, LANES), bf16)] * 4,
        compiler_params=pltpu.CompilerParams(vmem_limit_bytes=VMEM_LIMIT),
        cost_estimate=cost(160 * quarter * LANES, 72 * quarter * LANES),
    )(squares, mean, *states)


def states_kernel(squares, mean, master, first, second, *outs):
    values = adam_update(mean[...], master[...], first[...], second[...], clip_of(squares))
    for out, value in zip(outs, values):
        out[...] = value


def new_states(squares, mean, states):
    rows = mean.shape[0]
    whole = pl.BlockSpec(squares.shape, lambda i: (0, 0))
    block = pl.BlockSpec((2 * BLOCK, LANES), lambda i: (i, 0))
    return pl.pallas_call(
        states_kernel,
        grid=(rows // BLOCK // 2,),
        in_specs=[whole, block, block, block, block],
        out_specs=[block] * 3,
        out_shape=[jax.ShapeDtypeStruct((rows, LANES), f32)] * 3,
        compiler_params=pltpu.CompilerParams(vmem_limit_bytes=VMEM_LIMIT),
        cost_estimate=cost(20 * rows * LANES, 28 * rows * LANES),
    )(squares, mean, *states)


DIMS = {"zA": (Z, 1), "zB": (Z, 3), "xA": (X, 1), "xB": (X, 3)}
ORDERS = (("zA", "xA", "zB", "xB"), ("xA", "zB", "xB", "zA"), ("zB", "xB", "zA", "xA"), ("xB", "zA", "xA", "zB"))


def partner(value, dim):
    axis, mask = DIMS[dim]
    return lax.ppermute(value, axis, [(i, i ^ mask) for i in range(4)])


def join_kernel(one, two, out):
    size = one.shape[0]
    for i in range(size):
        out[i] = one[i]
        out[size + i] = two[i]


def join(one, two):
    here = pl.BlockSpec(memory_space=pltpu.VMEM)
    return pl.pallas_call(
        join_kernel,
        in_specs=[here, here],
        out_specs=here,
        out_shape=jax.ShapeDtypeStruct((2 * one.shape[0],) + one.shape[1:], one.dtype),
        compiler_params=pltpu.CompilerParams(vmem_limit_bytes=VMEM_LIMIT),
        cost_estimate=cost(0, 4 * one.size),
    )(one, two)


def masks_of(order):
    found = [(0, 0)]
    for dim in order:
        axis, mask = DIMS[dim]
        found += [(mz ^ mask, mx) if axis == Z else (mz, mx ^ mask) for mz, mx in found]
    return found


def set_kernel(jobs, n_parts, *refs):
    parts, out, sems = refs[:n_parts], refs[-2], refs[-1]
    z, x = lax.axis_index(Z), lax.axis_index(X)
    copies = []
    for k, (part, entry, chain, mz, mx) in enumerate(jobs):
        target = out.at[lax.bitwise_xor(z, mz), lax.bitwise_xor(x, mx), chain]
        copies.append(pltpu.make_async_copy(parts[part].at[entry], target, sems.at[k]))
    for copy in copies:
        copy.start()
    for copy in copies:
        copy.wait()


def set_blocks(out, parts, jobs, shape):
    extra = [] if out is None else [out]
    any_ = pl.BlockSpec(memory_space=pl.ANY)
    return pl.pallas_call(
        functools.partial(set_kernel, jobs, len(parts)),
        in_specs=[any_] * (len(parts) + len(extra)),
        out_specs=any_,
        scratch_shapes=[pltpu.SemaphoreType.DMA((len(jobs),))],
        out_shape=jax.ShapeDtypeStruct(shape, bf16),
        input_output_aliases={} if out is None else {len(parts): 0},
        compiler_params=pltpu.CompilerParams(vmem_limit_bytes=VMEM_LIMIT),
        cost_estimate=cost(0, 4 * sum(p.size for p in parts)),
    )(*parts, *extra)


def gather_blocks(blocks):
    held = [b[None] for b in blocks]
    for step in range(3):
        sent = [partner(h, order[step]) for h, order in zip(held, ORDERS)]
        held = [join(h, s) for h, s in zip(held, sent)]
    sent = [partner(h, order[3]) for h, order in zip(held, ORDERS)]
    shape = (4, 4, 4) + blocks[0].shape
    masks = [masks_of(order) for order in ORDERS]
    out = set_blocks(None, held, [(c, e, c) + masks[c][e] for c in range(4) for e in range(8)], shape)
    for c in range(4):
        out = set_blocks(out, [sent[c]], [(0, e, c) + masks[c][8 + e] for e in range(8)], shape)
    return out


def shards(local_grads, master_weights, first_moment, second_moment):
    layers, flat = local_grads.shape[2:]
    rows = layers * flat // LANES // 16
    halves = rows // 2, rows // 2
    z, x = lax.axis_index(Z), lax.axis_index(X)

    def to_rows(value):
        return value.reshape(layers, -1, LANES).transpose(1, 0, 2).reshape(-1, LANES)

    def from_rows(value):
        return value.reshape(-1, layers, LANES).transpose(1, 0, 2).reshape(1, layers, -1)

    pieces = to_rows(local_grads[0, 0]).reshape(4, 4, rows, LANES)
    states = [to_rows(s[0]) for s in (master_weights, first_moment, second_moment)]
    sends = pick(pieces, z, x, halves)
    axes = (Z, Z, X, X)
    ways = (1, 3, 1, 3)
    got = [shift(v, axis, by) for v, axis, by in zip(sends, axes, ways)]
    far = [shift(v[4:], axis, by).reshape(4, -1, LANES) for v, axis, by in zip(got, axes, ways)]
    own_a, own_b = own_pieces(pieces, halves)
    base_a = base_sum(own_a, got[0], got[1])
    base_b = base_sum(own_b, got[2], got[3])
    low_a, high_a = far_sum(X, base_a, far[0], far[1])
    low_b, high_b = far_sum(Z, base_b, far[2], far[3])
    low_a, high_a = shift(low_a, X, 1), shift(high_a, X, 3)
    low_b, high_b = shift(low_b, Z, 1), shift(high_b, Z, 3)
    next_a, last_a = near_sum(X, base_a, far[0], far[1], low_a, high_a)
    next_b, last_b = near_sum(Z, base_b, far[2], far[3], low_b, high_b)
    here_a, here_b = here_sum(base_a, far[0], far[1], base_b, far[2], far[3])
    parts_a = here_a, shift(next_a, X, 1), shift(last_a, X, 3)
    parts_b = here_b, shift(next_b, Z, 1), shift(last_b, Z, 3)
    devices = lax.axis_size((Z, X, Y, CORE))
    mean, squares = last_sum(parts_a, parts_b, devices)
    squares = lax.all_to_all(squares, (Z, X, Y, CORE), 0, 0, tiled=True)

    blocks = new_params(squares, mean, states)
    outs = [from_rows(o) for o in new_states(squares, mean, states)]
    out = gather_blocks(blocks)
    return (from_rows(out.reshape(-1, LANES)), *outs)


def solution(mesh):
    torus = Mesh(mesh.devices.reshape(4, 4, 4, 2), (Z, X, Y, CORE))
    dp, expert = (Z, X), (Y, CORE)
    return jax.shard_map(
        shards,
        mesh=torus,
        in_specs=(P(dp, expert, None, None), P(expert, None, dp), P(expert, None, dp), P(expert, None, dp)),
        out_specs=(P(expert, None, None), P(expert, None, dp), P(expert, None, dp), P(expert, None, dp)),
        check_vma=False,
    )
```

```python
import functools

import jax
import jax.numpy as jnp
from jax import lax
from jax.experimental import pallas as pl
from jax.experimental.pallas import tpu as pltpu
from jax.sharding import Mesh
from jax.sharding import PartitionSpec as P

Z, X, Y, CORE = "z", "x", "y", "core"
beta_first = 0.9
beta_second = 0.95
correct_first = 1.0 - 0.9**10
correct_second = 1.0 - 0.95**10
learn_rate = 0.05
decay_rate = 0.1
clip_limit = 1.0
tiny_eps = 1e-08
norm_eps = 1e-06

LANES = 128
BLOCK = 256
VMEM_LIMIT = 12 * 2**20
f32, bf16 = jnp.float32, jnp.bfloat16


def shift(value, axis, by):
    size = lax.axis_size(axis)
    return lax.ppermute(value, axis, [(i, (i + by) % size) for i in range(size)])


def cost(flops, moved):
    return pl.CostEstimate(flops=flops, bytes_accessed=moved, transcendentals=0)


def pick_kernel(at_z, at_x, pieces, *refs):
    outs, sems = refs[:4], refs[4]
    z, x = at_z[0], at_x[0]
    half_a = outs[0].shape[1]
    copies = []
    for k, (out, along_z, by) in enumerate(zip(outs, (True, True, False, False), (1, 3, 1, 3))):
        half = out.shape[1]
        quarter = half // 2
        me = z if along_z else x
        low = 0 if along_z else half_a
        far_low = low if by == 1 else low + quarter
        near, far = lax.rem(me + by, 4), lax.rem(me + 2, 4)
        rows = pl.ds(low, half)
        piece = pieces.at[near, :, rows] if along_z else pieces.at[:, near, rows]
        copies.append(pltpu.make_async_copy(piece, out.at[pl.ds(0, 4)], sems.at[k, 0]))
        for j in range(4):
            rows = pl.ds(far_low, quarter)
            piece = pieces.at[far, j, rows] if along_z else pieces.at[j, far, rows]
            target = out.at[4 + j // 2, pl.ds(j % 2 * quarter, quarter)]
            copies.append(pltpu.make_async_copy(piece, target, sems.at[k, 1 + j]))
    for copy in copies:
        copy.start()
    for copy in copies:
        copy.wait()


def pick(pieces, z, x, halves):
    any_ = pl.BlockSpec(memory_space=pl.ANY)
    return pl.pallas_call(
        pick_kernel,
        grid_spec=pltpu.PrefetchScalarGridSpec(
            num_scalar_prefetch=2,
            grid=(),
            in_specs=[any_],
            out_specs=[any_] * 4,
            scratch_shapes=[pltpu.SemaphoreType.DMA((4, 5))],
        ),
        out_shape=[jax.ShapeDtypeStruct((6, half, LANES), bf16) for half in halves for _ in range(2)],
        compiler_params=pltpu.CompilerParams(vmem_limit_bytes=VMEM_LIMIT),
        cost_estimate=cost(0, 48 * sum(halves) * LANES),
    )(z.reshape(1), x.reshape(1), pltpu.with_memory_space_constraint(pieces, pltpu.HBM))


def own_kernel(pieces, out_a, out_b, sems):
    half_a, half_b = out_a.shape[1], out_b.shape[1]
    z, x = lax.axis_index(Z), lax.axis_index(X)
    copies = [
        pltpu.make_async_copy(pieces.at[z, :, pl.ds(0, half_a)], out_a, sems.at[0]),
        pltpu.make_async_copy(pieces.at[:, x, pl.ds(half_a, half_b)], out_b, sems.at[1]),
    ]
    for copy in copies:
        copy.start()
    for copy in copies:
        copy.wait()


def own_pieces(pieces, halves):
    any_ = pl.BlockSpec(memory_space=pl.ANY)
    return pl.pallas_call(
        own_kernel,
        in_specs=[any_],
        out_specs=[any_] * 2,
        scratch_shapes=[pltpu.SemaphoreType.DMA((2,))],
        out_shape=[jax.ShapeDtypeStruct((4, half, LANES), bf16) for half in halves],
        compiler_params=pltpu.CompilerParams(vmem_limit_bytes=VMEM_LIMIT),
        cost_estimate=cost(0, 16 * sum(halves) * LANES),
    )(pltpu.with_memory_space_constraint(pieces, pltpu.HBM))


def base_kernel(own, behind, ahead, out):
    for j in range(4):

        @chunks_of(out.shape[1])
        def _(rows):
            out[j, rows] = own[j, rows].astype(f32) + behind[j, rows].astype(f32) + ahead[j, rows].astype(f32)


def base_sum(own, behind, ahead):
    here = pl.BlockSpec(memory_space=pltpu.VMEM)
    return pl.pallas_call(
        base_kernel,
        in_specs=[here] * 3,
        out_specs=here,
        out_shape=jax.ShapeDtypeStruct(own.shape, f32),
        compiler_params=pltpu.CompilerParams(vmem_limit_bytes=VMEM_LIMIT),
        cost_estimate=cost(2 * own.size, 60 * own.size),
    )(own, behind, ahead)


def chunks_of(size, *starts):
    step = max(n for n in (64, 48, 32, 16) if size % n == 0)

    def run(body):
        @pl.loop(0, size // step)
        def _(i):
            body(*(pl.ds(pl.multiple_of(at + i * step, 16), step) for at in (0, *starts)))

    return run


def far_sum_kernel(axis, base, far_low, far_high, low, high):
    quarter = low.shape[0]
    at = lax.rem(lax.axis_index(axis) + 2, 4)

    @chunks_of(quarter, quarter)
    def _(rows, upper):
        low[rows] = base[at, rows] + far_low[at, rows].astype(f32)
        high[rows] = base[at, upper] + far_high[at, rows].astype(f32)


def far_sum(axis, base, far_low, far_high):
    quarter = far_low.shape[1]
    here = pl.BlockSpec(memory_space=pltpu.VMEM)
    return pl.pallas_call(
        functools.partial(far_sum_kernel, axis),
        in_specs=[here] * 3,
        out_specs=[here] * 2,
        out_shape=[jax.ShapeDtypeStruct((quarter, LANES), f32)] * 2,
        compiler_params=pltpu.CompilerParams(vmem_limit_bytes=VMEM_LIMIT),
        cost_estimate=cost(2 * quarter * LANES, 20 * quarter * LANES),
    )(base, far_low, far_high)


def near_sum_kernel(axis, base, far_low, far_high, came_low, came_high, to_next, to_last):
    quarter = came_low.shape[0]
    after = lax.rem(lax.axis_index(axis) + 1, 4)
    before = lax.rem(lax.axis_index(axis) + 3, 4)

    @chunks_of(quarter, quarter)
    def _(rows, upper):
        to_next[rows] = base[after, rows] + far_low[after, rows].astype(f32) + came_low[rows]
        to_next[upper] = base[after, upper] + far_high[after, rows].astype(f32)
        to_last[rows] = base[before, rows] + far_low[before, rows].astype(f32)
        to_last[upper] = base[before, upper] + far_high[before, rows].astype(f32) + came_high[rows]


def near_sum(axis, base, far_low, far_high, came_low, came_high):
    quarter = far_low.shape[1]
    here = pl.BlockSpec(memory_space=pltpu.VMEM)
    return pl.pallas_call(
        functools.partial(near_sum_kernel, axis),
        in_specs=[here] * 5,
        out_specs=[here] * 2,
        out_shape=[jax.ShapeDtypeStruct((2 * quarter, LANES), f32)] * 2,
        compiler_params=pltpu.CompilerParams(vmem_limit_bytes=VMEM_LIMIT),
        cost_estimate=cost(10 * quarter * LANES, 48 * quarter * LANES),
    )(base, far_low, far_high, came_low, came_high)


def here_sum_kernel(*refs):
    for axis, (base, far_low, far_high), out in zip((X, Z), (refs[:3], refs[3:6]), refs[6:]):
        quarter = far_low.shape[1]
        at = lax.axis_index(axis)

        @chunks_of(quarter, quarter)
        def _(rows, upper):
            out[rows] = base[at, rows] + far_low[at, rows].astype(f32)
            out[upper] = base[at, upper] + far_high[at, rows].astype(f32)


def here_sum(base_a, low_a, high_a, base_b, low_b, high_b):
    here = pl.BlockSpec(memory_space=pltpu.VMEM)
    return pl.pallas_call(
        here_sum_kernel,
        in_specs=[here] * 6,
        out_specs=[here] * 2,
        out_shape=[jax.ShapeDtypeStruct(base.shape[1:], f32) for base in (base_a, base_b)],
        compiler_params=pltpu.CompilerParams(vmem_limit_bytes=VMEM_LIMIT),
        cost_estimate=cost(base_a.size // 2, 5 * base_a.size),
    )(base_a, low_a, high_a, base_b, low_b, high_b)


def last_sum_kernel(*refs):
    parts_a, parts_b, (mean, squares, held) = refs[:3], refs[3:6], refs[6:]
    half = parts_a[0].shape[0]
    held[...] = jnp.zeros_like(held)

    @chunks_of(half, half)
    def _(rows, upper):
        for parts, target in ((parts_a, rows), (parts_b, upper)):
            total = (parts[0][rows] + parts[1][rows] + parts[2][rows]) * (1.0 / 16.0)
            mean[target] = total
            held[...] += total * total

    total = jnp.sum(held[...], axis=0, keepdims=True)
    squares[...] = jnp.broadcast_to(total, squares.shape)


def last_sum(parts_a, parts_b, devices):
    rows = parts_a[0].shape[0] + parts_b[0].shape[0]
    here = pl.BlockSpec(memory_space=pltpu.VMEM)
    return pl.pallas_call(
        last_sum_kernel,
        in_specs=[here] * 6,
        out_specs=[here] * 2,
        out_shape=[jax.ShapeDtypeStruct((rows, LANES), f32), jax.ShapeDtypeStruct((devices, LANES), f32)],
        scratch_shapes=[pltpu.VMEM((64, LANES), f32)],
        compiler_params=pltpu.CompilerParams(vmem_limit_bytes=VMEM_LIMIT),
        cost_estimate=cost(8 * rows * LANES, 20 * rows * LANES),
    )(*parts_a, *parts_b)


def adam_update(gradient, master, first, second, clip_factor):
    scaled = clip_factor * gradient
    new_first = beta_first * first + (1.0 - beta_first) * scaled
    new_second = beta_second * second + (1.0 - beta_second) * scaled * scaled
    direction = (new_first * (1.0 / correct_first)) / (jnp.sqrt(new_second * (1.0 / correct_second)) + tiny_eps)
    new_master = (1.0 - learn_rate * decay_rate) * master - learn_rate * direction
    return (new_master, new_first, new_second)


def clip_of(squares):
    total = jnp.sum(jnp.sum(squares[...], axis=0, keepdims=True), axis=1, keepdims=True)
    return jnp.minimum(1.0, clip_limit / (jnp.sqrt(total) + norm_eps))


def params_kernel(squares, mean, master, first, second, *outs):
    clip_factor = clip_of(squares)
    size = outs[0].shape[0]
    for at, out in enumerate(outs):

        @chunks_of(size, at * size)
        def _(target, rows):
            new_master, _, _ = adam_update(mean[rows], master[rows], first[rows], second[rows], clip_factor)
            out[target] = new_master.astype(bf16)


def new_params(squares, mean, states):
    quarter = mean.shape[0] // 4
    here = pl.BlockSpec(memory_space=pltpu.VMEM)
    return pl.pallas_call(
        params_kernel,
        in_specs=[here] * 5,
        out_specs=[here] * 4,
        out_shape=[jax.ShapeDtypeStruct((quarter, LANES), bf16)] * 4,
        compiler_params=pltpu.CompilerParams(vmem_limit_bytes=VMEM_LIMIT),
        cost_estimate=cost(160 * quarter * LANES, 72 * quarter * LANES),
    )(squares, mean, *states)


def states_kernel(squares, mean, master, first, second, *outs):
    values = adam_update(mean[...], master[...], first[...], second[...], clip_of(squares))
    for out, value in zip(outs, values):
        out[...] = value


def new_states(squares, mean, states):
    rows = mean.shape[0]
    whole = pl.BlockSpec(squares.shape, lambda i: (0, 0))
    block = pl.BlockSpec((2 * BLOCK, LANES), lambda i: (i, 0))
    return pl.pallas_call(
        states_kernel,
        grid=(rows // BLOCK // 2,),
        in_specs=[whole, block, block, block, block],
        out_specs=[block] * 3,
        out_shape=[jax.ShapeDtypeStruct((rows, LANES), f32)] * 3,
        compiler_params=pltpu.CompilerParams(vmem_limit_bytes=VMEM_LIMIT),
        cost_estimate=cost(20 * rows * LANES, 28 * rows * LANES),
    )(squares, mean, *states)


DIMS = {"zA": (Z, 1), "zB": (Z, 3), "xA": (X, 1), "xB": (X, 3)}
ORDERS = (("zA", "xA", "zB", "xB"), ("xA", "zB", "xB", "zA"), ("zB", "xB", "zA", "xA"), ("xB", "zA", "xA", "zB"))


def partner(value, dim):
    axis, mask = DIMS[dim]
    return lax.ppermute(value, axis, [(i, i ^ mask) for i in range(4)])


def join_kernel(one, two, out):
    size = one.shape[0]
    for i in range(size):
        out[i] = one[i]
        out[size + i] = two[i]


def join(one, two):
    here = pl.BlockSpec(memory_space=pltpu.VMEM)
    return pl.pallas_call(
        join_kernel,
        in_specs=[here, here],
        out_specs=here,
        out_shape=jax.ShapeDtypeStruct((2 * one.shape[0],) + one.shape[1:], one.dtype),
        compiler_params=pltpu.CompilerParams(vmem_limit_bytes=VMEM_LIMIT),
        cost_estimate=cost(0, 4 * one.size),
    )(one, two)


def masks_of(order):
    found = [(0, 0)]
    for dim in order:
        axis, mask = DIMS[dim]
        found += [(mz ^ mask, mx) if axis == Z else (mz, mx ^ mask) for mz, mx in found]
    return found


def set_kernel(jobs, n_parts, *refs):
    parts, out, sems = refs[:n_parts], refs[-2], refs[-1]
    z, x = lax.axis_index(Z), lax.axis_index(X)
    copies = []
    for k, (part, entry, chain, mz, mx) in enumerate(jobs):
        target = out.at[lax.bitwise_xor(z, mz), lax.bitwise_xor(x, mx), chain]
        copies.append(pltpu.make_async_copy(parts[part].at[entry], target, sems.at[k]))
    for copy in copies:
        copy.start()
    for copy in copies:
        copy.wait()


def set_blocks(out, parts, jobs, shape):
    extra = [] if out is None else [out]
    any_ = pl.BlockSpec(memory_space=pl.ANY)
    return pl.pallas_call(
        functools.partial(set_kernel, jobs, len(parts)),
        in_specs=[any_] * (len(parts) + len(extra)),
        out_specs=any_,
        scratch_shapes=[pltpu.SemaphoreType.DMA((len(jobs),))],
        out_shape=jax.ShapeDtypeStruct(shape, bf16),
        input_output_aliases={} if out is None else {len(parts): 0},
        compiler_params=pltpu.CompilerParams(vmem_limit_bytes=VMEM_LIMIT),
        cost_estimate=cost(0, 4 * sum(p.size for p in parts)),
    )(*parts, *extra)


def gather_blocks(blocks):
    held = [b[None] for b in blocks]
    for step in range(3):
        sent = [partner(h, order[step]) for h, order in zip(held, ORDERS)]
        held = [join(h, s) for h, s in zip(held, sent)]
    sent = [partner(h, order[3]) for h, order in zip(held, ORDERS)]
    shape = (4, 4, 4) + blocks[0].shape
    masks = [masks_of(order) for order in ORDERS]
    out = set_blocks(None, held, [(c, e, c) + masks[c][e] for c in range(4) for e in range(8)], shape)
    for c in range(4):
        out = set_blocks(out, [sent[c]], [(0, e, c) + masks[c][8 + e] for e in range(8)], shape)
    return out


def shards(local_grads, master_weights, first_moment, second_moment):
    layers, flat = local_grads.shape[2:]
    rows = layers * flat // LANES // 16
    halves = rows // 2, rows // 2
    z, x = lax.axis_index(Z), lax.axis_index(X)

    def to_rows(value):
        return value.reshape(layers, -1, LANES).transpose(1, 0, 2).reshape(-1, LANES)

    def from_rows(value):
        return value.reshape(-1, layers, LANES).transpose(1, 0, 2).reshape(1, layers, -1)

    pieces = to_rows(local_grads[0, 0]).reshape(4, 4, rows, LANES)
    states = [to_rows(s[0]) for s in (master_weights, first_moment, second_moment)]
    sends = pick(pieces, z, x, halves)
    axes = (Z, Z, X, X)
    ways = (1, 3, 1, 3)
    got = [shift(v, axis, by) for v, axis, by in zip(sends, axes, ways)]
    far = [shift(v[4:], axis, by).reshape(4, -1, LANES) for v, axis, by in zip(got, axes, ways)]
    own_a, own_b = own_pieces(pieces, halves)
    base_a = base_sum(own_a, got[0], got[1])
    base_b = base_sum(own_b, got[2], got[3])
    low_a, high_a = far_sum(X, base_a, far[0], far[1])
    low_b, high_b = far_sum(Z, base_b, far[2], far[3])
    low_a, high_a = shift(low_a, X, 1), shift(high_a, X, 3)
    low_b, high_b = shift(low_b, Z, 1), shift(high_b, Z, 3)
    next_a, last_a = near_sum(X, base_a, far[0], far[1], low_a, high_a)
    next_b, last_b = near_sum(Z, base_b, far[2], far[3], low_b, high_b)
    here_a, here_b = here_sum(base_a, far[0], far[1], base_b, far[2], far[3])
    parts_a = here_a, shift(next_a, X, 1), shift(last_a, X, 3)
    parts_b = here_b, shift(next_b, Z, 1), shift(last_b, Z, 3)
    devices = lax.axis_size((Z, X, Y, CORE))
    mean, squares = last_sum(parts_a, parts_b, devices)
    squares = lax.all_to_all(squares, (Z, X, Y, CORE), 0, 0, tiled=True)

    blocks = new_params(squares, mean, states)
    outs = [from_rows(o) for o in new_states(squares, mean, states)]
    out = gather_blocks(blocks)
    return (from_rows(out.reshape(-1, LANES)), *outs)


def solution(mesh):
    torus = Mesh(mesh.devices.reshape(4, 4, 4, 2), (Z, X, Y, CORE))
    dp, expert = (Z, X), (Y, CORE)
    return jax.shard_map(
        shards,
        mesh=torus,
        in_specs=(P(dp, expert, None, None), P(expert, None, dp), P(expert, None, dp), P(expert, None, dp)),
        out_specs=(P(expert, None, None), P(expert, None, dp), P(expert, None, dp), P(expert, None, dp)),
        check_vma=False,
    )
```

```python
import functools

import jax
import jax.numpy as jnp
from jax import lax
from jax.experimental import pallas as pl
from jax.experimental.pallas import tpu as pltpu
from jax.sharding import Mesh
from jax.sharding import PartitionSpec as P

Z, X, Y, CORE = "z", "x", "y", "core"
beta_first = 0.9
beta_second = 0.95
correct_first = 1.0 - 0.9**10
correct_second = 1.0 - 0.95**10
learn_rate = 0.05
decay_rate = 0.1
clip_limit = 1.0
tiny_eps = 1e-08
norm_eps = 1e-06

LANES = 128
BLOCK = 256
VMEM_LIMIT = 12 * 2**20
f32, bf16 = jnp.float32, jnp.bfloat16


def shift(value, axis, by):
    size = lax.axis_size(axis)
    return lax.ppermute(value, axis, [(i, (i + by) % size) for i in range(size)])


def cost(flops, moved):
    return pl.CostEstimate(flops=flops, bytes_accessed=moved, transcendentals=0)


def pick_kernel(at_z, at_x, pieces, *refs):
    outs, sems = refs[:4], refs[4]
    z, x = at_z[0], at_x[0]
    half_a = outs[0].shape[1]
    copies = []
    for k, (out, along_z, by) in enumerate(zip(outs, (True, True, False, False), (1, 3, 1, 3))):
        half = out.shape[1]
        quarter = half // 2
        me = z if along_z else x
        low = 0 if along_z else half_a
        far_low = low if by == 1 else low + quarter
        near, far = lax.rem(me + by, 4), lax.rem(me + 2, 4)
        rows = pl.ds(low, half)
        piece = pieces.at[near, :, rows] if along_z else pieces.at[:, near, rows]
        copies.append(pltpu.make_async_copy(piece, out.at[pl.ds(0, 4)], sems.at[k, 0]))
        for j in range(4):
            rows = pl.ds(far_low, quarter)
            piece = pieces.at[far, j, rows] if along_z else pieces.at[j, far, rows]
            target = out.at[4 + j // 2, pl.ds(j % 2 * quarter, quarter)]
            copies.append(pltpu.make_async_copy(piece, target, sems.at[k, 1 + j]))
    for copy in copies:
        copy.start()
    for copy in copies:
        copy.wait()


def pick(pieces, z, x, halves):
    any_ = pl.BlockSpec(memory_space=pl.ANY)
    return pl.pallas_call(
        pick_kernel,
        grid_spec=pltpu.PrefetchScalarGridSpec(
            num_scalar_prefetch=2,
            grid=(),
            in_specs=[any_],
            out_specs=[any_] * 4,
            scratch_shapes=[pltpu.SemaphoreType.DMA((4, 5))],
        ),
        out_shape=[jax.ShapeDtypeStruct((6, half, LANES), bf16) for half in halves for _ in range(2)],
        compiler_params=pltpu.CompilerParams(vmem_limit_bytes=VMEM_LIMIT),
        cost_estimate=cost(0, 48 * sum(halves) * LANES),
    )(z.reshape(1), x.reshape(1), pltpu.with_memory_space_constraint(pieces, pltpu.HBM))


def own_kernel(pieces, out_a, out_b, sems):
    half_a, half_b = out_a.shape[1], out_b.shape[1]
    z, x = lax.axis_index(Z), lax.axis_index(X)
    copies = [
        pltpu.make_async_copy(pieces.at[z, :, pl.ds(0, half_a)], out_a, sems.at[0]),
        pltpu.make_async_copy(pieces.at[:, x, pl.ds(half_a, half_b)], out_b, sems.at[1]),
    ]
    for copy in copies:
        copy.start()
    for copy in copies:
        copy.wait()


def own_pieces(pieces, halves):
    any_ = pl.BlockSpec(memory_space=pl.ANY)
    return pl.pallas_call(
        own_kernel,
        in_specs=[any_],
        out_specs=[any_] * 2,
        scratch_shapes=[pltpu.SemaphoreType.DMA((2,))],
        out_shape=[jax.ShapeDtypeStruct((4, half, LANES), bf16) for half in halves],
        compiler_params=pltpu.CompilerParams(vmem_limit_bytes=VMEM_LIMIT),
        cost_estimate=cost(0, 16 * sum(halves) * LANES),
    )(pltpu.with_memory_space_constraint(pieces, pltpu.HBM))


def base_kernel(own, behind, ahead, out):
    for j in range(4):

        @chunks_of(out.shape[1])
        def _(rows):
            out[j, rows] = own[j, rows].astype(f32) + behind[j, rows].astype(f32) + ahead[j, rows].astype(f32)


def base_sum(own, behind, ahead):
    here = pl.BlockSpec(memory_space=pltpu.VMEM)
    return pl.pallas_call(
        base_kernel,
        in_specs=[here] * 3,
        out_specs=here,
        out_shape=jax.ShapeDtypeStruct(own.shape, f32),
        compiler_params=pltpu.CompilerParams(vmem_limit_bytes=VMEM_LIMIT),
        cost_estimate=cost(2 * own.size, 60 * own.size),
    )(own, behind, ahead)


def chunks_of(size, *starts):
    step = max(n for n in (128, 64, 48, 32, 16) if size % n == 0)

    def run(body):
        @pl.loop(0, size // step)
        def _(i):
            body(*(pl.ds(pl.multiple_of(at + i * step, 16), step) for at in (0, *starts)))

    return run


def far_sum_kernel(axis, base, far_low, far_high, low, high):
    quarter = low.shape[0]
    at = lax.rem(lax.axis_index(axis) + 2, 4)

    @chunks_of(quarter, quarter)
    def _(rows, upper):
        low[rows] = base[at, rows] + far_low[at, rows].astype(f32)
        high[rows] = base[at, upper] + far_high[at, rows].astype(f32)


def far_sum(axis, base, far_low, far_high):
    quarter = far_low.shape[1]
    here = pl.BlockSpec(memory_space=pltpu.VMEM)
    return pl.pallas_call(
        functools.partial(far_sum_kernel, axis),
        in_specs=[here] * 3,
        out_specs=[here] * 2,
        out_shape=[jax.ShapeDtypeStruct((quarter, LANES), f32)] * 2,
        compiler_params=pltpu.CompilerParams(vmem_limit_bytes=VMEM_LIMIT),
        cost_estimate=cost(2 * quarter * LANES, 20 * quarter * LANES),
    )(base, far_low, far_high)


def near_sum_kernel(axis, base, far_low, far_high, came_low, came_high, to_next, to_last):
    quarter = came_low.shape[0]
    after = lax.rem(lax.axis_index(axis) + 1, 4)
    before = lax.rem(lax.axis_index(axis) + 3, 4)

    @chunks_of(quarter, quarter)
    def _(rows, upper):
        to_next[rows] = base[after, rows] + far_low[after, rows].astype(f32) + came_low[rows]
        to_next[upper] = base[after, upper] + far_high[after, rows].astype(f32)
        to_last[rows] = base[before, rows] + far_low[before, rows].astype(f32)
        to_last[upper] = base[before, upper] + far_high[before, rows].astype(f32) + came_high[rows]


def near_sum(axis, base, far_low, far_high, came_low, came_high):
    quarter = far_low.shape[1]
    here = pl.BlockSpec(memory_space=pltpu.VMEM)
    return pl.pallas_call(
        functools.partial(near_sum_kernel, axis),
        in_specs=[here] * 5,
        out_specs=[here] * 2,
        out_shape=[jax.ShapeDtypeStruct((2 * quarter, LANES), f32)] * 2,
        compiler_params=pltpu.CompilerParams(vmem_limit_bytes=VMEM_LIMIT),
        cost_estimate=cost(10 * quarter * LANES, 48 * quarter * LANES),
    )(base, far_low, far_high, came_low, came_high)


def here_sum_kernel(*refs):
    for axis, (base, far_low, far_high), out in zip((X, Z), (refs[:3], refs[3:6]), refs[6:]):
        quarter = far_low.shape[1]
        at = lax.axis_index(axis)

        @chunks_of(quarter, quarter)
        def _(rows, upper):
            out[rows] = base[at, rows] + far_low[at, rows].astype(f32)
            out[upper] = base[at, upper] + far_high[at, rows].astype(f32)


def here_sum(base_a, low_a, high_a, base_b, low_b, high_b):
    here = pl.BlockSpec(memory_space=pltpu.VMEM)
    return pl.pallas_call(
        here_sum_kernel,
        in_specs=[here] * 6,
        out_specs=[here] * 2,
        out_shape=[jax.ShapeDtypeStruct(base.shape[1:], f32) for base in (base_a, base_b)],
        compiler_params=pltpu.CompilerParams(vmem_limit_bytes=VMEM_LIMIT),
        cost_estimate=cost(base_a.size // 2, 5 * base_a.size),
    )(base_a, low_a, high_a, base_b, low_b, high_b)


def last_sum_kernel(*refs):
    parts_a, parts_b, (mean, squares, held) = refs[:3], refs[3:6], refs[6:]
    half = parts_a[0].shape[0]
    held[...] = jnp.zeros_like(held)

    @chunks_of(half, half)
    def _(rows, upper):
        for parts, target in ((parts_a, rows), (parts_b, upper)):
            total = (parts[0][rows] + parts[1][rows] + parts[2][rows]) * (1.0 / 16.0)
            mean[target] = total
            held[...] += total * total

    total = jnp.sum(held[...], axis=0, keepdims=True)
    squares[...] = jnp.broadcast_to(total, squares.shape)


def last_sum(parts_a, parts_b, devices):
    rows = parts_a[0].shape[0] + parts_b[0].shape[0]
    here = pl.BlockSpec(memory_space=pltpu.VMEM)
    return pl.pallas_call(
        last_sum_kernel,
        in_specs=[here] * 6,
        out_specs=[here] * 2,
        out_shape=[jax.ShapeDtypeStruct((rows, LANES), f32), jax.ShapeDtypeStruct((devices, LANES), f32)],
        scratch_shapes=[pltpu.VMEM((128, LANES), f32)],
        compiler_params=pltpu.CompilerParams(vmem_limit_bytes=VMEM_LIMIT),
        cost_estimate=cost(8 * rows * LANES, 20 * rows * LANES),
    )(*parts_a, *parts_b)


def adam_update(gradient, master, first, second, clip_factor):
    scaled = clip_factor * gradient
    new_first = beta_first * first + (1.0 - beta_first) * scaled
    new_second = beta_second * second + (1.0 - beta_second) * scaled * scaled
    direction = (new_first * (1.0 / correct_first)) / (jnp.sqrt(new_second * (1.0 / correct_second)) + tiny_eps)
    new_master = (1.0 - learn_rate * decay_rate) * master - learn_rate * direction
    return (new_master, new_first, new_second)


def clip_of(squares):
    total = jnp.sum(jnp.sum(squares[...], axis=0, keepdims=True), axis=1, keepdims=True)
    return jnp.minimum(1.0, clip_limit / (jnp.sqrt(total) + norm_eps))


def params_kernel(squares, mean, master, first, second, *outs):
    clip_factor = clip_of(squares)
    size = outs[0].shape[0]
    for at, out in enumerate(outs):

        @chunks_of(size, at * size)
        def _(target, rows):
            new_master, _, _ = adam_update(mean[rows], master[rows], first[rows], second[rows], clip_factor)
            out[target] = new_master.astype(bf16)


def new_params(squares, mean, states):
    quarter = mean.shape[0] // 4
    here = pl.BlockSpec(memory_space=pltpu.VMEM)
    return pl.pallas_call(
        params_kernel,
        in_specs=[here] * 5,
        out_specs=[here] * 4,
        out_shape=[jax.ShapeDtypeStruct((quarter, LANES), bf16)] * 4,
        compiler_params=pltpu.CompilerParams(vmem_limit_bytes=VMEM_LIMIT),
        cost_estimate=cost(160 * quarter * LANES, 72 * quarter * LANES),
    )(squares, mean, *states)


def states_kernel(squares, mean, master, first, second, *outs):
    values = adam_update(mean[...], master[...], first[...], second[...], clip_of(squares))
    for out, value in zip(outs, values):
        out[...] = value


def new_states(squares, mean, states):
    rows = mean.shape[0]
    whole = pl.BlockSpec(squares.shape, lambda i: (0, 0))
    block = pl.BlockSpec((2 * BLOCK, LANES), lambda i: (i, 0))
    return pl.pallas_call(
        states_kernel,
        grid=(rows // BLOCK // 2,),
        in_specs=[whole, block, block, block, block],
        out_specs=[block] * 3,
        out_shape=[jax.ShapeDtypeStruct((rows, LANES), f32)] * 3,
        compiler_params=pltpu.CompilerParams(vmem_limit_bytes=VMEM_LIMIT),
        cost_estimate=cost(20 * rows * LANES, 28 * rows * LANES),
    )(squares, mean, *states)


DIMS = {"zA": (Z, 1), "zB": (Z, 3), "xA": (X, 1), "xB": (X, 3)}
ORDERS = (("zA", "xA", "zB", "xB"), ("xA", "zB", "xB", "zA"), ("zB", "xB", "zA", "xA"), ("xB", "zA", "xA", "zB"))


def partner(value, dim):
    axis, mask = DIMS[dim]
    return lax.ppermute(value, axis, [(i, i ^ mask) for i in range(4)])


def join_kernel(one, two, out):
    size = one.shape[0]
    for i in range(size):
        out[i] = one[i]
        out[size + i] = two[i]


def join(one, two):
    here = pl.BlockSpec(memory_space=pltpu.VMEM)
    return pl.pallas_call(
        join_kernel,
        in_specs=[here, here],
        out_specs=here,
        out_shape=jax.ShapeDtypeStruct((2 * one.shape[0],) + one.shape[1:], one.dtype),
        compiler_params=pltpu.CompilerParams(vmem_limit_bytes=VMEM_LIMIT),
        cost_estimate=cost(0, 4 * one.size),
    )(one, two)


def masks_of(order):
    found = [(0, 0)]
    for dim in order:
        axis, mask = DIMS[dim]
        found += [(mz ^ mask, mx) if axis == Z else (mz, mx ^ mask) for mz, mx in found]
    return found


def set_kernel(jobs, n_parts, *refs):
    parts, out, sems = refs[:n_parts], refs[-2], refs[-1]
    z, x = lax.axis_index(Z), lax.axis_index(X)
    copies = []
    for k, (part, entry, chain, mz, mx) in enumerate(jobs):
        target = out.at[lax.bitwise_xor(z, mz), lax.bitwise_xor(x, mx), chain]
        copies.append(pltpu.make_async_copy(parts[part].at[entry], target, sems.at[k]))
    for copy in copies:
        copy.start()
    for copy in copies:
        copy.wait()


def set_blocks(out, parts, jobs, shape):
    extra = [] if out is None else [out]
    any_ = pl.BlockSpec(memory_space=pl.ANY)
    return pl.pallas_call(
        functools.partial(set_kernel, jobs, len(parts)),
        in_specs=[any_] * (len(parts) + len(extra)),
        out_specs=any_,
        scratch_shapes=[pltpu.SemaphoreType.DMA((len(jobs),))],
        out_shape=jax.ShapeDtypeStruct(shape, bf16),
        input_output_aliases={} if out is None else {len(parts): 0},
        compiler_params=pltpu.CompilerParams(vmem_limit_bytes=VMEM_LIMIT),
        cost_estimate=cost(0, 4 * sum(p.size for p in parts)),
    )(*parts, *extra)


def gather_blocks(blocks):
    held = [b[None] for b in blocks]
    for step in range(3):
        sent = [partner(h, order[step]) for h, order in zip(held, ORDERS)]
        held = [join(h, s) for h, s in zip(held, sent)]
    sent = [partner(h, order[3]) for h, order in zip(held, ORDERS)]
    shape = (4, 4, 4) + blocks[0].shape
    masks = [masks_of(order) for order in ORDERS]
    out = set_blocks(None, held, [(c, e, c) + masks[c][e] for c in range(4) for e in range(8)], shape)
    for c in range(4):
        out = set_blocks(out, [sent[c]], [(0, e, c) + masks[c][8 + e] for e in range(8)], shape)
    return out


def shards(local_grads, master_weights, first_moment, second_moment):
    layers, flat = local_grads.shape[2:]
    rows = layers * flat // LANES // 16
    halves = rows // 2, rows // 2
    z, x = lax.axis_index(Z), lax.axis_index(X)

    def to_rows(value):
        return value.reshape(layers, -1, LANES).transpose(1, 0, 2).reshape(-1, LANES)

    def from_rows(value):
        return value.reshape(-1, layers, LANES).transpose(1, 0, 2).reshape(1, layers, -1)

    pieces = to_rows(local_grads[0, 0]).reshape(4, 4, rows, LANES)
    states = [to_rows(s[0]) for s in (master_weights, first_moment, second_moment)]
    sends = pick(pieces, z, x, halves)
    axes = (Z, Z, X, X)
    ways = (1, 3, 1, 3)
    got = [shift(v, axis, by) for v, axis, by in zip(sends, axes, ways)]
    far = [shift(v[4:], axis, by).reshape(4, -1, LANES) for v, axis, by in zip(got, axes, ways)]
    own_a, own_b = own_pieces(pieces, halves)
    base_a = base_sum(own_a, got[0], got[1])
    base_b = base_sum(own_b, got[2], got[3])
    low_a, high_a = far_sum(X, base_a, far[0], far[1])
    low_b, high_b = far_sum(Z, base_b, far[2], far[3])
    low_a, high_a = shift(low_a, X, 1), shift(high_a, X, 3)
    low_b, high_b = shift(low_b, Z, 1), shift(high_b, Z, 3)
    next_a, last_a = near_sum(X, base_a, far[0], far[1], low_a, high_a)
    next_b, last_b = near_sum(Z, base_b, far[2], far[3], low_b, high_b)
    here_a, here_b = here_sum(base_a, far[0], far[1], base_b, far[2], far[3])
    parts_a = here_a, shift(next_a, X, 1), shift(last_a, X, 3)
    parts_b = here_b, shift(next_b, Z, 1), shift(last_b, Z, 3)
    devices = lax.axis_size((Z, X, Y, CORE))
    mean, squares = last_sum(parts_a, parts_b, devices)
    squares = lax.all_to_all(squares, (Z, X, Y, CORE), 0, 0, tiled=True)

    blocks = new_params(squares, mean, states)
    outs = [from_rows(o) for o in new_states(squares, mean, states)]
    out = gather_blocks(blocks)
    return (from_rows(out.reshape(-1, LANES)), *outs)


def solution(mesh):
    torus = Mesh(mesh.devices.reshape(4, 4, 4, 2), (Z, X, Y, CORE))
    dp, expert = (Z, X), (Y, CORE)
    return jax.shard_map(
        shards,
        mesh=torus,
        in_specs=(P(dp, expert, None, None), P(expert, None, dp), P(expert, None, dp), P(expert, None, dp)),
        out_specs=(P(expert, None, None), P(expert, None, dp), P(expert, None, dp), P(expert, None, dp)),
        check_vma=False,
    )
```
